32 devices in a mesh: ty: 2 (over x), tx: 16 (over z, y, core).
Axes of the slice: x: 2, y: 2, z: 4, core: 2. Of those that a mesh axis runs over, the one named last changes fastest.
Arguments:
- object_field: float32 [2, 256, 2048], P(None, 'ty', 'tx'), may hold values from -40 to 40
- probe: float32 [2, 4, 128, 128], replicated, may hold values from -3 to 3
- intensities: float32 [2, 16, 3, 128, 128], P('ty', 'tx'), may hold values from 0.25 to 16
- positions: int32 [2, 16, 3, 2], P('ty', 'tx'), may hold values from 0 to 128
Outputs:
- object_out: float32 [2, 256, 2048], P(None, 'ty', 'tx')
- probe_out: float32 [2, 4, 128, 128], replicated
The draws below stay inside these ranges and needn't reach their ends.
All inputs are finite; a program needn't handle non-finite values.
Results may differ from the reference program's by a relative error of at most 0.0003.
Values sent between devices are 32-bit elements; how exact they have to be, the bound alone decides.
No kernel may reach another device: no remote copies, remote signals or barrier semaphores. Data moves between devices by JAX's collectives and lax.ppermute only.
A program may use at most 64 MiB of HBM per device.

```python
import math
import jax
import jax.numpy as jnp
from jax import lax

WIN = 128
MODES = 4
TILE = 128
SCANS = 3
ROUNDS = 2
NY = 256
NX = 2048
N_TY = 2
N_TX = 16


def draw_object_field(key, part):
    key_base, key_rows, key_cols = jax.random.split(key, 3)
    row_pos = jnp.arange(NY, dtype=jnp.float32) / NY
    col_pos = jnp.arange(NX, dtype=jnp.float32) / NX
    row_factor = jnp.exp(jax.random.uniform(key_rows, (NY,), jnp.float32, 0.0, jnp.log(3.2)))
    col_factor = jnp.exp(jax.random.uniform(key_cols, (NX,), jnp.float32, 0.0, jnp.log(3.2)))
    base = jnp.clip(jax.random.normal(key_base, (2, NY, NX), jnp.float32), -4.0, 4.0)
    trend = jnp.sqrt(0.5 + row_pos[:, None] + col_pos[None, :])
    scaled = 0.5 * base * trend[None] * row_factor[None, :, None] * col_factor[None, None, :]
    return scaled.astype(jnp.float32)


def place_ends(values, key, least, high):
    shape = values.shape
    spot = [jax.random.randint(jax.random.fold_in(key, axis), (), 0, shape[axis]) for axis in range(len(shape))]
    values = values.at[tuple(spot)].set(least)
    longest = shape.index(max(shape))
    spot[longest] = (spot[longest] + 1) % shape[longest]
    return values.at[tuple(spot)].set(high)


def levels(rng, shape, cuts, smallest, largest):
    gain, own = 1.0, jax.random.fold_in(rng, 6)
    for axis_at, shards_of in cuts:
        draws = jnp.exp(jax.random.uniform(jax.random.fold_in(own, axis_at), (shards_of,), jnp.float32, smallest / len(cuts), largest / len(cuts)))
        gain = gain * jnp.repeat(draws, shape[axis_at] // shards_of).reshape([-1 if axis == axis_at else 1 for axis in range(len(shape))])
    return gain


def scatter_about(stream_key, dims, width, bound, kind=jnp.bfloat16):
    return jnp.clip(width * jax.random.normal(stream_key, dims, jnp.float32), -bound, bound).astype(kind)


def setup_inputs(seed: int = 0) -> dict:
    key_list = jax.random.split(jax.random.key(seed), 5)
    return {
        "object_field": draw_object_field(jax.random.fold_in(key_list[4], 71), 0),
        "probe": scatter_about(key_list[1], (2, MODES, WIN, WIN), 0.5, 3.0, jnp.float32),
        "intensities": jnp.clip(jnp.exp(math.log(16.0) - 4.158883 * jax.random.uniform(key_list[2], (N_TY, N_TX, SCANS, WIN, WIN), jnp.float32) ** levels(key_list[2], (N_TY, N_TX, SCANS, WIN, WIN), ((0, 2), (1, 16)), -0.2, 0.2)), 0.25, 16.0),
        "positions": place_ends(jax.random.randint(key_list[3], (N_TY, N_TX, SCANS, 2), 0, TILE + 1), jax.random.fold_in(key_list[3], 1), 0, TILE).astype(jnp.int32),
    }


OBJECT_STEP = 0.1
PROBE_RELAX = 0.5

def reference(object_field, probe, intensities, positions):
    win_size = probe.shape[-1]
    margin = win_size // 2
    measured = jnp.sqrt(intensities)
    zero_index = jnp.zeros((), jnp.int32)
    for round_index in range(ROUNDS):
        padded = jnp.pad(object_field, ((0, 0), (margin, margin), (margin, margin)))
        probe_cplx = lax.complex(probe[0], probe[1])

        def visit_tile(item_index, loop_state):
            grad_grid, probe_grad, weight = loop_state
            item_int = jnp.asarray(item_index).astype(jnp.int32)
            tile_row = item_int // N_TX
            tile_col = item_int % N_TX
            tile_anchor = jnp.stack([tile_row * TILE, tile_col * TILE]).astype(jnp.int32)
            win_starts = (positions[tile_row, tile_col].astype(jnp.int32) + tile_anchor[None, :]).astype(jnp.int32)

            def cut_window(corner):
                return lax.dynamic_slice(padded, (zero_index, corner[0].astype(jnp.int32), corner[1].astype(jnp.int32)), (2, win_size, win_size))
            windows = jax.vmap(cut_window)(win_starts)
            win_cplx = lax.complex(windows[:, 0], windows[:, 1])
            exit_waves = probe_cplx[None] * win_cplx[:, None]
            far_field = jnp.fft.fft2(exit_waves, norm='ortho')
            far_power = lax.optimization_barrier(jnp.sum(jnp.real(far_field) ** 2 + jnp.imag(far_field) ** 2, axis=1))
            factor = measured[tile_row, tile_col] / jnp.sqrt(jnp.maximum(far_power, 1.0)) - 1.0
            back_field = jnp.fft.ifft2(far_field * factor[:, None], norm='ortho')
            obj_grad = lax.optimization_barrier(jnp.sum(jnp.conj(probe_cplx)[None] * back_field, axis=1))
            probe_grad = probe_grad + lax.optimization_barrier(jnp.sum(jnp.conj(win_cplx)[:, None] * back_field, axis=0))
            weight = weight + jnp.sum(windows * windows)

            def place(scan_index, grid_now):
                corner = win_starts[scan_index]
                start_tuple = (zero_index, corner[0].astype(jnp.int32), corner[1].astype(jnp.int32))
                previous = lax.dynamic_slice(grid_now, start_tuple, (2, win_size, win_size))
                grad_piece = jnp.stack([jnp.real(obj_grad[scan_index]), jnp.imag(obj_grad[scan_index])])
                return lax.dynamic_update_slice(grid_now, previous + grad_piece, start_tuple)
            grad_grid = lax.fori_loop(0, SCANS, place, grad_grid)
            return (grad_grid, probe_grad, weight)
        start_state = (jnp.zeros_like(padded), jnp.zeros_like(probe_cplx), jnp.zeros((), jnp.float32))
        grad_grid, probe_grad, weight = lax.fori_loop(0, N_TY * N_TX, visit_tile, start_state)
        new_object = object_field + OBJECT_STEP * grad_grid[:, margin:-margin, margin:-margin]
        probe_real = jnp.stack([jnp.real(probe_grad), jnp.imag(probe_grad)])
        probe = probe + PROBE_RELAX * win_size * win_size / weight * probe_real
        object_field = new_object
    return (object_field, probe)
```

```python
import functools

import jax
import jax.numpy as jnp
import numpy as np
from jax import lax
from jax.experimental import pallas as pl
from jax.experimental.pallas import tpu as pltpu
from jax.sharding import PartitionSpec as P

ROUNDS = 2
OBJECT_STEP = 0.1
PROBE_RELAX = 0.5
AXES = ("ty", "tx")
SUBLANES = 8
WEIGHT_ROWS = SUBLANES
F32 = jnp.float32
BF16 = jnp.bfloat16


def dft_blocks(win):
    line = np.arange(win, dtype=np.int64)
    angle = (line[:, None] * line[None, :] % win) * (2.0 * np.pi / win)
    c, s = np.cos(angle) / np.sqrt(win), np.sin(angle) / np.sqrt(win)
    full = np.block([[c, -s], [s, c]]).astype(np.float32)
    high = full.astype(jnp.bfloat16)
    low = (full - high.astype(np.float32)).astype(jnp.bfloat16)
    return np.stack([high, low]), np.stack([high.T, low.T])


def pairings(size):
    found = []
    for first in (0, 1):
        pairs = {}
        for low in range(first, size - 1, 2):
            pairs[low], pairs[low + 1] = low + 1, low
        if pairs:
            found.append(pairs)
    return found


def flat_pairs(pairs_y, pairs_x, n_ty, n_tx):
    out = []
    for y in range(n_ty):
        for x in range(n_tx):
            to_y = y if pairs_y is None else pairs_y.get(y)
            to_x = x if pairs_x is None else pairs_x.get(x)
            if to_y is not None and to_x is not None:
                out.append((y * n_tx + x, to_y * n_tx + to_x))
    return out


def xor_permute(x, mask, total):
    return lax.ppermute(x, AXES, [(i, i ^ mask) for i in range(total)])


def split(x):
    high = x.astype(BF16)
    return high, (x - high.astype(F32)).astype(BF16)


def product(a, b):
    (a_high, a_low), (b_high, b_low) = a, b
    dot = functools.partial(jnp.dot, preferred_element_type=F32)
    return dot(a_high, b_high) + (dot(a_low, b_high) + dot(a_high, b_low))


def lane_pick(width, margin, flag):
    lane = lax.broadcasted_iota(jnp.int32, (8, width), 1)
    below = jnp.where(lane < margin, 0, 1)
    return below == flag


def rowwise(mask, rows):
    return jnp.broadcast_to(mask[:1], (rows, mask.shape[1]))


def by_parity(odd, even_value, odd_value):
    return jnp.where(odd == 1, odd_value, even_value)


def compute(
    ext_ref, probe_ref, meas_ref, pos_ref, right_ref, left_ref, grid_ref, grad_ref, *, margin
):
    scans, win = meas_ref.shape[0], meas_ref.shape[1]
    modes = probe_ref.shape[1]
    width = 2 * win
    w_fwd = (right_ref[0], right_ref[1])
    l_fwd = (left_ref[0], left_ref[1])
    grid_ref[...] = jnp.zeros_like(grid_ref)
    weight = jnp.zeros((WEIGHT_ROWS, win), F32)
    for s in range(scans):
        r, c = pos_ref[s, 0], pos_ref[s, 1]
        turn = jnp.where(c <= margin, margin - c, margin + width - c)
        back = jnp.where(c >= margin, c - margin, c + width - margin)
        q = r % SUBLANES
        base = pl.multiple_of(r - q, SUBLANES)
        tall = win + SUBLANES
        lift = jnp.where(q == 0, 0, tall - q)

        def window(part):
            band = pltpu.roll(ext_ref[part, pl.ds(base, tall), :], turn, 1)[:, :win]
            return pltpu.roll(band, lift, 0)[:win]

        o_re, o_im = window(0), window(1)
        power = o_re * o_re + o_im * o_im
        weight = weight + jnp.sum(power.reshape(win // WEIGHT_ROWS, WEIGHT_ROWS, win), axis=0)
        rows = []
        for k in range(modes):
            p_re, p_im = probe_ref[0, k], probe_ref[1, k]
            rows.append(
                jnp.concatenate([p_re * o_re - p_im * o_im, p_re * o_im + p_im * o_re], axis=1)
            )
        y = product(split(jnp.concatenate(rows, axis=0)), w_fwd)
        y = jnp.concatenate(
            [
                jnp.concatenate([y[k * win : (k + 1) * win, :win] for k in range(modes)], axis=1),
                jnp.concatenate([y[k * win : (k + 1) * win, win:] for k in range(modes)], axis=1),
            ],
            axis=0,
        )
        far = product(l_fwd, split(y))
        square = far * far
        square = square[:win] + square[win:]
        total = square[:, :win]
        for k in range(1, modes):
            total = total + square[:, k * win : (k + 1) * win]
        ratio = jnp.sqrt(meas_ref[s]) * lax.rsqrt(jnp.maximum(total, 1.0)) - 1.0
        ratio = jnp.concatenate([ratio] * modes, axis=1)
        far = far * jnp.concatenate([ratio, ratio], axis=0)
        u = product(w_fwd, split(far))
        u = jnp.concatenate(
            [
                jnp.concatenate(
                    [u[:win, k * win : (k + 1) * win], u[win:, k * win : (k + 1) * win]], axis=1
                )
                for k in range(modes)
            ],
            axis=0,
        )
        chi = product(split(u), l_fwd)
        g_re = g_im = None
        for k in range(modes):
            p_re, p_im = probe_ref[0, k], probe_ref[1, k]
            c_re, c_im = chi[k * win : (k + 1) * win, :win], chi[k * win : (k + 1) * win, win:]
            a, b = p_re * c_re + p_im * c_im, p_re * c_im - p_im * c_re
            g_re, g_im = (a, b) if k == 0 else (g_re + a, g_im + b)
            a, b = o_re * c_re + o_im * c_im, o_re * c_im - o_im * c_re
            if s == 0:
                grad_ref[k], grad_ref[modes + k] = a, b
            else:
                grad_ref[k] += a
                grad_ref[modes + k] += b
        for part, g in ((0, g_re), (1, g_im)):
            g = pltpu.roll(jnp.concatenate([g, jnp.zeros((SUBLANES, win), F32)], axis=0), q, 0)
            g = jnp.concatenate([g, jnp.zeros_like(g)], axis=1)
            grid_ref[part, pl.ds(base, tall), :] += pltpu.roll(g, back, 1)
    return weight


def emit_halves(grad_ref, weight, keep_ref, send_ref, half):
    count, win = keep_ref.shape[0], grad_ref.shape[1]
    for j in range(count):
        keep_ref[j, :win, :] = grad_ref[half * count + j]
        send_ref[j, :win, :] = grad_ref[(1 - half) * count + j]
        keep_ref[j, win:, :] = weight
        send_ref[j, win:, :] = weight


def first_kernel(
    n_y, n_x, margin, pos_ref, obj_ref, probe_ref, meas_ref, right_ref, left_ref, *rest
):
    take = iter(rest)
    ty_refs = [next(take) for _ in range(n_y)]
    tx_refs = [next(take) for _ in range(n_x)]
    corner_refs = [[next(take) for _ in range(n_x)] for _ in range(n_y)]
    ext_ref, keep_ref, send_ref, grid_ref, *msg_refs, grad_ref = take
    tile = obj_ref.shape[-1]
    odd_y, odd_x = lax.axis_index("ty") % 2, lax.axis_index("tx") % 2
    pick = lane_pick(tile, margin, odd_x)

    def side(refs, part, rows):
        if not refs:
            return jnp.zeros((rows, tile), F32)
        other = refs[1][part] if len(refs) > 1 else jnp.zeros((rows, tile), F32)
        return jnp.where(rowwise(pick, rows), refs[0][part], other)

    for part in (0, 1):
        ext_ref[part, margin : margin + tile, :tile] = obj_ref[part]
        ext_ref[part, margin : margin + tile, tile:] = side(tx_refs, part, tile)
        bands = [
            jnp.concatenate([ty_refs[i][part], side(corner_refs[i], part, margin)], axis=1)
            for i in range(n_y)
        ]
        while len(bands) < 2:
            bands.append(jnp.zeros((margin, 2 * tile), F32))
        ext_ref[part, :margin, :] = by_parity(odd_y, bands[1], bands[0])
        ext_ref[part, margin + tile : 2 * tile, :] = by_parity(odd_y, bands[0], bands[1])
    weight = compute(
        ext_ref, probe_ref, meas_ref, pos_ref, right_ref, left_ref, grid_ref, grad_ref, margin=margin
    )
    emit_halves(grad_ref, weight, keep_ref, send_ref, odd_x)
    for i, ref in enumerate(msg_refs):
        high = jnp.where(odd_x == i, 1, 0)
        mask = rowwise(lane_pick(tile, margin, high), 2 * tile)
        for part in (0, 1):
            ref[part] = jnp.where(
                mask, grid_ref[part, : 2 * tile, :tile], grid_ref[part, : 2 * tile, tile:]
            )


def combined_probe(probe_ref, own_ref, other_ref, new_ref, half):
    count, win, modes = own_ref.shape[0], probe_ref.shape[-1], probe_ref.shape[1]
    weight = jnp.sum(own_ref[0, win:, :])
    scale = PROBE_RELAX * win * win / jnp.full((8, win), weight, F32)
    scale = jnp.broadcast_to(scale[:1], (win, win))
    for j in range(count):
        for ref, index in ((own_ref, half * count + j), (other_ref, (1 - half) * count + j)):
            part, k = index // modes, index % modes
            new_ref[part, k] = probe_ref[part, k] + scale * ref[j, :win, :]


def second_kernel(
    n_y, n_x, n_ty, n_tx, margin, pos_ref, old_ref, grid_old_ref, probe_ref, meas_ref, right_ref,
    left_ref, own_ref, other_ref, *rest
):
    take = iter(rest)
    tx_refs = [next(take) for _ in range(n_x)]
    ty_refs = [next(take) for _ in range(n_y)]
    tile_ref, new_ref, keep_ref, send_ref, grid_ref, ext_ref, grad_ref = take
    tile = probe_ref.shape[-1]
    at_y, at_x = lax.axis_index("ty"), lax.axis_index("tx")
    odd_y, odd_x = at_y % 2, at_x % 2
    combined_probe(probe_ref, own_ref, other_ref, new_ref, odd_x)
    row = lax.broadcasted_iota(jnp.int32, (2 * tile, 2 * tile), 0)
    lane = lax.broadcasted_iota(jnp.int32, (2 * tile, 2 * tile), 1)
    inside = (row >= jnp.where(at_y == 0, margin, 0)) & (
        row < jnp.where(at_y == n_ty - 1, margin + tile, 2 * tile)
    )
    inside &= (lane < jnp.where(at_x == n_tx - 1, tile, tile + margin)) | (
        lane >= jnp.where(at_x == 0, 2 * tile, tile + margin)
    )
    for part in (0, 1):
        total = grid_old_ref[part, : 2 * tile, :]
        if n_x:
            total = total + spread(tx_refs, part, odd_x, margin, tile)
        ext_ref[part, : 2 * tile, :] = total
        for i, ref in enumerate(ty_refs):
            start = pl.multiple_of(jnp.where(odd_y == i, tile, 0), tile)
            ext_ref[part, pl.ds(start, tile), :] += ref[part]
        step = jnp.where(inside, OBJECT_STEP * ext_ref[part, : 2 * tile, :], 0.0)
        ext_ref[part, : 2 * tile, :] = old_ref[part, : 2 * tile, :] + step
        tile_ref[part] = ext_ref[part, margin : margin + tile, :tile]
    weight = compute(
        ext_ref, new_ref, meas_ref, pos_ref, right_ref, left_ref, grid_ref, grad_ref, margin=margin
    )
    emit_halves(grad_ref, weight, keep_ref, send_ref, odd_x)


def spread(tx_refs, part, odd_x, margin, tile):
    rows = 2 * tile
    first = tx_refs[0][part]
    second = tx_refs[1][part] if len(tx_refs) > 1 else jnp.zeros((rows, tile), F32)
    low = rowwise(lane_pick(tile, margin, odd_x), rows)
    return jnp.concatenate(
        [jnp.where(low, second, first), jnp.where(low, first, second)], axis=1
    )


def last_kernel(n_y, n_x, margin, tile_ref, mid_ref, probe_ref, own_ref, other_ref, *rest):
    take = iter(rest)
    ty_refs = [next(take) for _ in range(n_y)]
    obj_ref, new_ref = take
    tile = probe_ref.shape[-1]
    odd_y, odd_x = lax.axis_index("ty") % 2, lax.axis_index("tx") % 2
    combined_probe(probe_ref, own_ref, other_ref, new_ref, odd_x)
    for part in (0, 1):
        obj_ref[part] = mid_ref[part, margin : margin + tile, :]
        for i, ref in enumerate(ty_refs):
            start = pl.multiple_of(jnp.where(odd_y == i, tile - margin, 0), margin)
            obj_ref[part, pl.ds(start, margin), :] += ref[part]
        obj_ref[part] = tile_ref[part] + OBJECT_STEP * obj_ref[part]


def call(kernel, outs, ins, scratch=()):
    smem = pl.BlockSpec(memory_space=pltpu.SMEM)
    vmem = pl.BlockSpec(memory_space=pltpu.VMEM)
    shapes = [jax.ShapeDtypeStruct(s, F32) for s in outs]
    return pl.pallas_call(
        kernel,
        out_shape=shapes,
        in_specs=[smem if x.dtype == jnp.int32 else vmem for x in ins],
        out_specs=[vmem] * len(outs),
        scratch_shapes=[pltpu.VMEM(s, F32) for s in scratch],
        compiler_params=pltpu.CompilerParams(vmem_limit_bytes=32 * 1024 * 1024),
    )(*ins)


def bit_of(me, bit):
    return (me >> bit) & 1


def masks_of(bits):
    return [sum(((m >> i) & 1) << b for i, b in enumerate(bits)) for m in range(1, 1 << len(bits))]


def local_index(me, bits):
    return sum(bit_of(me, b) << i for i, b in enumerate(bits))


def tree(values):
    while len(values) > 1:
        values = [a + b for a, b in zip(values[::2], values[1::2])] + values[len(values) & ~1 :]
    return values[0]


def scatter_sum(x, me, bits, total):
    here = local_index(me, bits)
    n = 1 << len(bits)
    x = x.reshape((n, x.shape[0] // n) + x.shape[1:])
    parts = [lax.dynamic_index_in_dim(x, here, 0, False)]
    for m, mask in enumerate(masks_of(bits), 1):
        parts.append(xor_permute(lax.dynamic_index_in_dim(x, here ^ m, 0, False), mask, total))
    return tree(parts)


def direct_sum(x, bits, total):
    return tree([x] + [xor_permute(x, mask, total) for mask in masks_of(bits)])


def gather(x, me, bits, total):
    here = local_index(me, bits)
    parts = jnp.stack([x] + [xor_permute(x, mask, total) for mask in masks_of(bits)])
    return jnp.concatenate(
        [lax.dynamic_index_in_dim(parts, here ^ j, 0, False) for j in range(1 << len(bits))]
    )


def summed_halves(keep, send, n_ty, n_tx):
    total = n_ty * n_tx
    me = lax.axis_index("ty") * n_tx + lax.axis_index("tx")
    levels = total.bit_length() - 1
    half = keep + xor_permute(send, 1, total)
    tx_bits = n_tx.bit_length() - 1
    bits = [b for b in (tx_bits, 1) if b < levels]
    rest = [b for b in range(1, levels) if b not in bits]
    half = scatter_sum(half, me, bits, total)
    for i in range(0, len(rest), 2):
        half = direct_sum(half, rest[i : i + 2], total)
    half = gather(half, me, bits, total)
    return half, xor_permute(half, 1, total)


def per_device(n_ty, n_tx, tables, object_field, probe, intensities, positions):
    win, modes = probe.shape[-1], probe.shape[1]
    margin, tile, scans = win // 2, object_field.shape[-1], positions.shape[2]
    spots = positions.reshape(scans, 2)
    measured = intensities.reshape(scans, win, win)
    right, left = (jnp.asarray(t) for t in tables)
    match_y, match_x = pairings(n_ty), pairings(n_tx)
    n_y, n_x = len(match_y), len(match_x)
    odd_y = lax.axis_index("ty") % 2

    def swap(x, pairs_y, pairs_x):
        return lax.ppermute(x, AXES, flat_pairs(pairs_y, pairs_x, n_ty, n_tx))

    def rows_for(x, i, count, low, high):
        start = jnp.where(odd_y == i, high, low)
        return lax.dynamic_slice_in_dim(x, start, count, 1)

    tx_in = [swap(object_field, None, px) for px in match_x]
    rims = [rows_for(object_field, i, margin, 0, tile - margin) for i in range(n_y)]
    ty_in = [swap(rims[i], py, None) for i, py in enumerate(match_y)]
    corners = [swap(rims[i], py, px) for i, py in enumerate(match_y) for px in match_x]

    half_shape = (modes, win + WEIGHT_ROWS, win)
    grid_shape = (2, 2 * tile + SUBLANES, 2 * tile)
    msg_shape = (2, 2 * tile, tile)
    ext, keep, send, grid, *msgs = call(
        functools.partial(first_kernel, n_y, n_x, margin),
        [grid_shape, half_shape, half_shape, grid_shape] + [msg_shape] * n_x,
        [spots, object_field, probe, measured, right, left, *ty_in, *tx_in, *corners],
        [(2 * modes, win, win)],
    )
    own, other = summed_halves(keep, send, n_ty, n_tx)
    tx_in = [swap(m, None, px) for m, px in zip(msgs, match_x)]
    odd_x = lax.axis_index("tx") % 2
    lane = lax.broadcasted_iota(jnp.int32, (1, 1, tile), 2)
    low = jnp.where(lane < margin, 0, 1) == odd_x
    second = tx_in[1] if n_x > 1 else jnp.zeros(msg_shape, F32)
    extra = jnp.concatenate(
        [jnp.where(low, second, tx_in[0]), jnp.where(low, tx_in[0], second)], axis=2
    ) if n_x else jnp.zeros((2, 2 * tile, 2 * tile), F32)
    wide = grid[:, : 2 * tile, :] + extra
    bands = [rows_for(wide, i, tile, 0, tile) for i in range(n_y)]
    ty_in = [swap(bands[i], py, None) for i, py in enumerate(match_y)]
    tile_mid, probe_mid, keep, send, grid = call(
        functools.partial(second_kernel, n_y, n_x, n_ty, n_tx, margin),
        [object_field.shape, probe.shape, half_shape, half_shape, grid_shape],
        [spots, ext, grid, probe, measured, right, left, own, other, *tx_in, *ty_in],
        [grid_shape, (2 * modes, win, win)],
    )
    own, other = summed_halves(keep, send, n_ty, n_tx)
    edge = grid[:, : 2 * tile, tile:]
    tx_in = [swap(edge, None, px) for px in match_x]
    mid = grid[:, : 2 * tile, :tile]
    if n_x:
        second = tx_in[1] if n_x > 1 else jnp.zeros(msg_shape, F32)
        mid = mid + jnp.where(low, second, tx_in[0])
    bands = [rows_for(mid, i, margin, 0, 2 * tile - margin) for i in range(n_y)]
    ty_in = [swap(bands[i], py, None) for i, py in enumerate(match_y)]
    return call(
        functools.partial(last_kernel, n_y, n_x, margin),
        [object_field.shape, probe.shape],
        [tile_mid, mid, probe_mid, own, other, *ty_in],
    )


def solution(mesh):
    n_ty, n_tx = mesh.shape["ty"], mesh.shape["tx"]
    placed = (P(None, "ty", "tx"), P(), P("ty", "tx", None, None, None), P("ty", "tx", None, None))

    def run(object_field, probe, intensities, positions):
        tables = dft_blocks(probe.shape[-1])
        return jax.shard_map(
            functools.partial(per_device, n_ty, n_tx, tables),
            mesh=mesh,
            in_specs=placed,
            out_specs=(P(None, "ty", "tx"), P()),
            check_vma=False,
        )(object_field, probe, intensities, positions)

    return run
```

```python
import functools

import jax
import jax.numpy as jnp
import numpy as np
from jax import lax
from jax.experimental import pallas as pl
from jax.experimental.pallas import tpu as pltpu
from jax.sharding import PartitionSpec as P

ROUNDS = 2
OBJECT_STEP = 0.1
PROBE_RELAX = 0.5
AXES = ("ty", "tx")
SUBLANES = 8
WEIGHT_ROWS = SUBLANES
F32 = jnp.float32
BF16 = jnp.bfloat16


def dft_table(win):
    line = np.arange(win, dtype=np.int64)
    angle = (line[:, None] * line[None, :] % win) * (2.0 * np.pi / win)
    full = (np.stack([np.cos(angle), np.sin(angle)]) / np.sqrt(win)).astype(np.float32)
    high = full.astype(jnp.bfloat16)
    low = (full - high.astype(np.float32)).astype(jnp.bfloat16)
    return np.concatenate([high, low])


def pairings(size):
    found = []
    for first in (0, 1):
        pairs = {}
        for low in range(first, size - 1, 2):
            pairs[low], pairs[low + 1] = low + 1, low
        if pairs:
            found.append(pairs)
    return found


def flat_pairs(pairs_y, pairs_x, n_ty, n_tx):
    out, alone = [], []
    for x in range(n_tx):
        for y in range(n_ty):
            to_y = y if pairs_y is None else pairs_y.get(y)
            to_x = x if pairs_x is None else pairs_x.get(x)
            if to_y is None or to_x is None:
                alone.append(y * n_tx + x)
            else:
                out.append((y * n_tx + x, to_y * n_tx + to_x))
    for a, b in zip(alone[::2], alone[1::2]):
        out += [(a, b), (b, a)]
    if len(alone) % 2:
        out.append((alone[-1], alone[-1]))
    return out


def if_paired(x, at, size, i):
    last = i + 2 * ((size - i) // 2)
    if i > 0:
        x = jnp.where(at >= i, x, 0.0)
    return jnp.where(at < last, x, 0.0) if last < size else x


def xor_permute(x, mask, total):
    return lax.ppermute(x, AXES, [(i, i ^ mask) for i in range(total)])


def split(x):
    high = x.astype(BF16)
    return high, (x - high.astype(F32)).astype(BF16)


def product(a, b):
    (a_high, a_low), (b_high, b_low) = a, b
    dot = functools.partial(jnp.dot, preferred_element_type=F32)
    return dot(a_high, b_high) + (dot(a_low, b_high) + dot(a_high, b_low))


def block(c, upper, lower):
    return jnp.concatenate(
        [jnp.concatenate([c, upper], axis=1), jnp.concatenate([lower, c], axis=1)], axis=0
    )


def lane_pick(width, margin, flag):
    lane = lax.broadcasted_iota(jnp.int32, (8, width), 1)
    below = jnp.where(lane < margin, 0, 1)
    return below == flag


def rowwise(mask, rows):
    return jnp.broadcast_to(mask[:1], (rows, mask.shape[1]))


def by_parity(odd, even_value, odd_value):
    return jnp.where(odd == 1, odd_value, even_value)


def compute(
    ext_ref, probe_ref, root_ref, pos_ref, table_ref, grid_ref, grad_ref, *, margin
):
    scans, win = root_ref.shape[0], root_ref.shape[1]
    modes = probe_ref.shape[1]
    width = 2 * win
    w_fwd = [block(table_ref[i], -table_ref[i + 1], table_ref[i + 1]) for i in (0, 2)]
    l_fwd = [block(table_ref[i], table_ref[i + 1], -table_ref[i + 1]) for i in (0, 2)]
    grid_ref[...] = jnp.zeros_like(grid_ref)
    weight = jnp.zeros((WEIGHT_ROWS, win), F32)
    for s in range(scans):
        r, c = pos_ref[s, 0], pos_ref[s, 1]
        turn = jnp.where(c <= margin, margin - c, margin + width - c)
        back = jnp.where(c >= margin, c - margin, c + width - margin)
        q = r % SUBLANES
        base = pl.multiple_of(r - q, SUBLANES)
        tall = win + SUBLANES
        lift = jnp.where(q == 0, 0, tall - q)

        def window(part):
            band = pltpu.roll(ext_ref[part, pl.ds(base, tall), :], turn, 1)[:, :win]
            return pltpu.roll(band, lift, 0)[:win]

        o_re, o_im = window(0), window(1)
        power = o_re * o_re + o_im * o_im
        weight = weight + jnp.sum(power.reshape(win // WEIGHT_ROWS, WEIGHT_ROWS, win), axis=0)
        rows = []
        for k in range(modes):
            p_re, p_im = probe_ref[0, k], probe_ref[1, k]
            rows.append(
                jnp.concatenate([p_re * o_re - p_im * o_im, p_re * o_im + p_im * o_re], axis=1)
            )
        y = product(split(jnp.concatenate(rows, axis=0)), w_fwd)
        y = jnp.concatenate(
            [
                jnp.concatenate([y[k * win : (k + 1) * win, :win] for k in range(modes)], axis=1),
                jnp.concatenate([y[k * win : (k + 1) * win, win:] for k in range(modes)], axis=1),
            ],
            axis=0,
        )
        far = product(l_fwd, split(y))
        square = far * far
        square = square[:win] + square[win:]
        total = square[:, :win]
        for k in range(1, modes):
            total = total + square[:, k * win : (k + 1) * win]
        ratio = root_ref[s] * lax.rsqrt(jnp.maximum(total, 1.0)) - 1.0
        ratio = jnp.concatenate([ratio] * modes, axis=1)
        far = far * jnp.concatenate([ratio, ratio], axis=0)
        u = product(w_fwd, split(far))
        u = jnp.concatenate(
            [
                jnp.concatenate(
                    [u[:win, k * win : (k + 1) * win], u[win:, k * win : (k + 1) * win]], axis=1
                )
                for k in range(modes)
            ],
            axis=0,
        )
        chi = product(split(u), l_fwd)
        g_re = g_im = None
        for k in range(modes):
            p_re, p_im = probe_ref[0, k], probe_ref[1, k]
            c_re, c_im = chi[k * win : (k + 1) * win, :win], chi[k * win : (k + 1) * win, win:]
            a, b = p_re * c_re + p_im * c_im, p_re * c_im - p_im * c_re
            g_re, g_im = (a, b) if k == 0 else (g_re + a, g_im + b)
            a, b = o_re * c_re + o_im * c_im, o_re * c_im - o_im * c_re
            if s == 0:
                grad_ref[k], grad_ref[modes + k] = a, b
            else:
                grad_ref[k] += a
                grad_ref[modes + k] += b
        for part, g in ((0, g_re), (1, g_im)):
            g = pltpu.roll(jnp.concatenate([g, jnp.zeros((SUBLANES, win), F32)], axis=0), q, 0)
            g = jnp.concatenate([g, jnp.zeros_like(g)], axis=1)
            grid_ref[part, pl.ds(base, tall), :] += pltpu.roll(g, back, 1)
    return weight


def emit_halves(grad_ref, weight, keep_ref, send_ref, half):
    count, win = keep_ref.shape[0], grad_ref.shape[1]
    for j in range(count):
        keep_ref[j, :win, :] = grad_ref[half * count + j]
        send_ref[j, :win, :] = grad_ref[(1 - half) * count + j]
        keep_ref[j, win:, :] = weight
        send_ref[j, win:, :] = weight


def prepare_kernel(probe_ref, meas_ref, table_ref, probe_out, root_ref, table_out):
    probe_out[...] = probe_ref[...]
    root_ref[...] = jnp.sqrt(meas_ref[...])
    table_out[...] = table_ref[...]


def first_kernel(n_ty, n_tx, n_y, n_x, margin, pos_ref, obj_ref, probe_ref, root_ref, table_ref, *rest):
    take = iter(rest)
    ty_refs = [next(take) for _ in range(n_y)]
    tx_refs = [next(take) for _ in range(n_x)]
    corner_refs = [[next(take) for _ in range(n_x)] for _ in range(n_y)]
    ext_ref, keep_ref, send_ref, grid_ref, *msg_refs, grad_ref = take
    tile = obj_ref.shape[-1]
    at_y, at_x = lax.axis_index("ty"), lax.axis_index("tx")
    odd_y, odd_x = at_y % 2, at_x % 2
    pick = lane_pick(tile, margin, odd_x)

    def side(refs, part, rows):
        both = [if_paired(ref[part], at_x, n_tx, i) for i, ref in enumerate(refs)]
        both += [jnp.zeros((rows, tile), F32)] * (2 - n_x)
        return jnp.where(rowwise(pick, rows), both[0], both[1])

    for part in (0, 1):
        ext_ref[part, margin : margin + tile, :tile] = obj_ref[part]
        ext_ref[part, margin : margin + tile, tile:] = side(tx_refs, part, tile)
        bands = [
            if_paired(
                jnp.concatenate([ty_refs[i][part], side(corner_refs[i], part, margin)], axis=1),
                at_y, n_ty, i,
            )
            for i in range(n_y)
        ]
        bands += [jnp.zeros((margin, 2 * tile), F32)] * (2 - n_y)
        ext_ref[part, :margin, :] = by_parity(odd_y, bands[1], bands[0])
        ext_ref[part, margin + tile : 2 * tile, :] = by_parity(odd_y, bands[0], bands[1])
    weight = compute(
        ext_ref, probe_ref, root_ref, pos_ref, table_ref, grid_ref, grad_ref, margin=margin
    )
    emit_halves(grad_ref, weight, keep_ref, send_ref, odd_x)
    for i, ref in enumerate(msg_refs):
        high = jnp.where(odd_x == i, 1, 0)
        mask = rowwise(lane_pick(tile, margin, high), 2 * tile)
        for part in (0, 1):
            ref[part] = jnp.where(
                mask, grid_ref[part, : 2 * tile, :tile], grid_ref[part, : 2 * tile, tile:]
            )


def combined_probe(probe_ref, own_ref, other_ref, new_ref, half):
    count, win, modes = own_ref.shape[0], probe_ref.shape[-1], probe_ref.shape[1]
    weight = jnp.sum(own_ref[0, win:, :])
    scale = PROBE_RELAX * win * win / jnp.full((8, win), weight, F32)
    scale = jnp.broadcast_to(scale[:1], (win, win))
    for j in range(count):
        for ref, index in ((own_ref, half * count + j), (other_ref, (1 - half) * count + j)):
            part, k = index // modes, index % modes
            new_ref[part, k] = probe_ref[part, k] + scale * ref[j, :win, :]


def second_kernel(
    n_ty, n_tx, n_y, n_x, margin, pos_ref, old_ref, grid_old_ref, probe_ref, root_ref, table_ref,
    own_ref, other_ref, *rest
):
    take = iter(rest)
    tx_refs = [next(take) for _ in range(n_x)]
    ty_refs = [next(take) for _ in range(n_y)]
    tile_ref, new_ref, keep_ref, send_ref, grid_ref, edge_ref, ext_ref, grad_ref = take
    tile = probe_ref.shape[-1]
    at_y, at_x = lax.axis_index("ty"), lax.axis_index("tx")
    odd_y, odd_x = at_y % 2, at_x % 2
    combined_probe(probe_ref, own_ref, other_ref, new_ref, odd_x)
    row = lax.broadcasted_iota(jnp.int32, (2 * tile, 2 * tile), 0)
    lane = lax.broadcasted_iota(jnp.int32, (2 * tile, 2 * tile), 1)
    inside = (row >= jnp.where(at_y == 0, margin, 0)) & (
        row < jnp.where(at_y == n_ty - 1, margin + tile, 2 * tile)
    )
    inside &= (lane < jnp.where(at_x == n_tx - 1, tile, tile + margin)) | (
        lane >= jnp.where(at_x == 0, 2 * tile, tile + margin)
    )
    for part in (0, 1):
        total = grid_old_ref[part, : 2 * tile, :]
        if n_x:
            total = total + spread(tx_refs, part, at_x, n_tx, margin, tile)
        ext_ref[part, : 2 * tile, :] = total
        for i, ref in enumerate(ty_refs):
            start = pl.multiple_of(jnp.where(odd_y == i, tile, 0), tile)
            ext_ref[part, pl.ds(start, tile), :] += if_paired(ref[part], at_y, n_ty, i)
        step = jnp.where(inside, OBJECT_STEP * ext_ref[part, : 2 * tile, :], 0.0)
        ext_ref[part, : 2 * tile, :] = old_ref[part, : 2 * tile, :] + step
        tile_ref[part] = ext_ref[part, margin : margin + tile, :tile]
    weight = compute(
        ext_ref, new_ref, root_ref, pos_ref, table_ref, grid_ref, grad_ref, margin=margin
    )
    emit_halves(grad_ref, weight, keep_ref, send_ref, odd_x)
    edge_ref[...] = grid_ref[:, : 2 * tile, tile:]


def spread(tx_refs, part, at_x, n_tx, margin, tile):
    rows = 2 * tile
    both = [if_paired(ref[part], at_x, n_tx, i) for i, ref in enumerate(tx_refs)]
    both += [jnp.zeros((rows, tile), F32)] * (2 - len(both))
    low = rowwise(lane_pick(tile, margin, at_x % 2), rows)
    return jnp.concatenate(
        [jnp.where(low, both[1], both[0]), jnp.where(low, both[0], both[1])], axis=1
    )


def last_kernel(n_ty, n_y, margin, tile_ref, mid_ref, probe_ref, own_ref, other_ref, *rest):
    take = iter(rest)
    ty_refs = [next(take) for _ in range(n_y)]
    obj_ref, new_ref = take
    tile = probe_ref.shape[-1]
    at_y = lax.axis_index("ty")
    combined_probe(probe_ref, own_ref, other_ref, new_ref, lax.axis_index("tx") % 2)
    for part in (0, 1):
        obj_ref[part] = mid_ref[part, margin : margin + tile, :]
        for i, ref in enumerate(ty_refs):
            start = pl.multiple_of(jnp.where(at_y % 2 == i, tile - margin, 0), margin)
            obj_ref[part, pl.ds(start, margin), :] += if_paired(ref[part], at_y, n_ty, i)
        obj_ref[part] = tile_ref[part] + OBJECT_STEP * obj_ref[part]


def call(kernel, outs, ins, scratch=()):
    smem = pl.BlockSpec(memory_space=pltpu.SMEM)
    vmem = pl.BlockSpec(memory_space=pltpu.VMEM)
    shapes = [s if hasattr(s, "dtype") else jax.ShapeDtypeStruct(s, F32) for s in outs]
    return pl.pallas_call(
        kernel,
        out_shape=shapes,
        in_specs=[smem if x.dtype == jnp.int32 else vmem for x in ins],
        out_specs=[vmem] * len(outs),
        scratch_shapes=[pltpu.VMEM(s, F32) for s in scratch],
        compiler_params=pltpu.CompilerParams(vmem_limit_bytes=16 * 1024 * 1024),
    )(*ins)


def bit_of(me, bit):
    return (me >> bit) & 1


def masks_of(bits):
    return [sum(((m >> i) & 1) << b for i, b in enumerate(bits)) for m in range(1, 1 << len(bits))]


def local_index(me, bits):
    return sum(bit_of(me, b) << i for i, b in enumerate(bits))


def tree(values):
    while len(values) > 1:
        values = [a + b for a, b in zip(values[::2], values[1::2])] + values[len(values) & ~1 :]
    return values[0]


def scatter_sum(x, me, bits, total):
    here = local_index(me, bits)
    n = 1 << len(bits)
    x = x.reshape((n, x.shape[0] // n) + x.shape[1:])
    parts = [lax.dynamic_index_in_dim(x, here, 0, False)]
    for m, mask in enumerate(masks_of(bits), 1):
        parts.append(xor_permute(lax.dynamic_index_in_dim(x, here ^ m, 0, False), mask, total))
    return tree(parts)


def direct_sum(x, bits, total):
    return tree([x] + [xor_permute(x, mask, total) for mask in masks_of(bits)])


def gather(x, me, bits, total):
    here = local_index(me, bits)
    parts = jnp.stack([x] + [xor_permute(x, mask, total) for mask in masks_of(bits)])
    return jnp.concatenate(
        [lax.dynamic_index_in_dim(parts, here ^ j, 0, False) for j in range(1 << len(bits))]
    )


def summed_halves(keep, send, n_ty, n_tx, columns, rows, early):
    total = n_ty * n_tx
    me = lax.axis_index("ty") * n_tx + lax.axis_index("tx")
    levels = total.bit_length() - 1
    tx_bits = n_tx.bit_length() - 1
    bits = [b for b in (tx_bits, 1) if b < levels]
    rest = [b for b in range(1, levels) if b not in bits]
    half = keep + xor_permute(send, 1, total)
    across = columns()
    half = scatter_sum(half, me, bits, total)
    if early:
        half, across = lax.optimization_barrier((half, across))
        along = rows(across)
    for i in range(0, len(rest), 2):
        half = direct_sum(half, rest[i : i + 2], total)
    if early:
        half, along = lax.optimization_barrier((half, along))
    else:
        half, across = lax.optimization_barrier((half, across))
        along = rows(across)
    half = gather(half, me, bits, total)
    if not early:
        half, along = lax.optimization_barrier((half, along))
    return half, xor_permute(half, 1, total), across, along


def per_device(n_ty, n_tx, table, object_field, probe, intensities, positions):
    win, modes = probe.shape[-1], probe.shape[1]
    margin, tile, scans = win // 2, object_field.shape[-1], positions.shape[2]
    spots = positions.reshape(scans, 2)
    measured = intensities.reshape(scans, win, win)
    match_y, match_x = pairings(n_ty), pairings(n_tx)
    n_y, n_x = len(match_y), len(match_x)
    odd_y = lax.axis_index("ty") % 2

    def swap(x, pairs_y, pairs_x):
        return lax.ppermute(x, AXES, flat_pairs(pairs_y, pairs_x, n_ty, n_tx))

    def rows_for(x, i, count, low, high):
        start = jnp.where(odd_y == i, high, low)
        return lax.dynamic_slice_in_dim(x, start, count, 1)

    tx_in = [swap(object_field, None, px) for px in match_x]
    rims = [rows_for(object_field, i, margin, 0, tile - margin) for i in range(n_y)]
    ty_in = [swap(rims[i], py, None) for i, py in enumerate(match_y)]
    corners = []
    for i, py in enumerate(match_y):
        corners += [swap(ty_in[i], None, px) for px in match_x[:1]]
        corners += [swap(rims[i], py, px) for px in match_x[1:]]

    shape_of = lambda x: jax.ShapeDtypeStruct(x.shape, x.dtype)
    ready = (probe, measured, jnp.asarray(table))
    ready = call(prepare_kernel, [shape_of(x) for x in ready], ready)
    (tx_in, ty_in, corners), (probe, root, table) = lax.optimization_barrier(
        ((tx_in, ty_in, corners), tuple(ready))
    )

    at_x = lax.axis_index("tx")
    lane = lax.broadcasted_iota(jnp.int32, (1, 1, tile), 2)
    low = jnp.where(lane < margin, 0, 1) == at_x % 2

    def joined(messages):
        both = [if_paired(m, at_x, n_tx, i) for i, m in enumerate(messages)]
        both += [jnp.zeros_like(messages[0])] * (2 - n_x)
        return jnp.where(low, both[1], both[0]), jnp.where(low, both[0], both[1])

    half_shape = (modes, win + WEIGHT_ROWS, win)
    grid_shape = (2, 2 * tile + SUBLANES, 2 * tile)
    msg_shape = (2, 2 * tile, tile)
    ext, keep, send, grid, *msgs = call(
        functools.partial(first_kernel, n_ty, n_tx, n_y, n_x, margin),
        [grid_shape, half_shape, half_shape, grid_shape] + [msg_shape] * n_x,
        [spots, object_field, probe, root, table, *ty_in, *tx_in, *corners],
        [(2 * modes, win, win)],
    )

    def columns():
        return [swap(m, None, px) for m, px in zip(msgs, match_x)]

    def rows(across):
        wide = grid[:, : 2 * tile, :]
        if n_x:
            wide = wide + jnp.concatenate(joined(across), axis=2)
        bands = [rows_for(wide, i, tile, 0, tile) for i in range(n_y)]
        return [swap(bands[i], py, None) for i, py in enumerate(match_y)]

    own, other, tx_in, ty_in = summed_halves(keep, send, n_ty, n_tx, columns, rows, True)
    tile_mid, probe_mid, keep, send, grid_last, edge = call(
        functools.partial(second_kernel, n_ty, n_tx, n_y, n_x, margin),
        [object_field.shape, probe.shape, half_shape, half_shape, grid_shape, msg_shape],
        [spots, ext, grid, probe, root, table, own, other, *tx_in, *ty_in],
        [grid_shape, (2 * modes, win, win)],
    )

    def columns():
        return [swap(edge, None, px) for px in match_x]

    def middle(across):
        mid = grid_last[:, : 2 * tile, :tile]
        return mid + joined(across)[0] if n_x else mid

    def rows(across):
        mid = middle(across)
        bands = [rows_for(mid, i, margin, 0, 2 * tile - margin) for i in range(n_y)]
        return [swap(bands[i], py, None) for i, py in enumerate(match_y)]

    own, other, tx_in, ty_in = summed_halves(keep, send, n_ty, n_tx, columns, rows, False)
    return call(
        functools.partial(last_kernel, n_ty, n_y, margin),
        [object_field.shape, probe.shape],
        [tile_mid, middle(tx_in), probe_mid, own, other, *ty_in],
    )


def solution(mesh):
    n_ty, n_tx = mesh.shape["ty"], mesh.shape["tx"]
    placed = (P(None, "ty", "tx"), P(), P("ty", "tx", None, None, None), P("ty", "tx", None, None))

    def run(object_field, probe, intensities, positions):
        table = dft_table(probe.shape[-1])
        return jax.shard_map(
            functools.partial(per_device, n_ty, n_tx, table),
            mesh=mesh,
            in_specs=placed,
            out_specs=(P(None, "ty", "tx"), P()),
            check_vma=False,
        )(object_field, probe, intensities, positions)

    return run
```

```python
import functools

import jax
import jax.numpy as jnp
import numpy as np
from jax import lax
from jax.experimental import pallas as pl
from jax.experimental.pallas import tpu as pltpu
from jax.sharding import PartitionSpec as P

ROUNDS = 2
OBJECT_STEP = 0.1
PROBE_RELAX = 0.5
AXES = ("ty", "tx")
SUBLANES = 8
WEIGHT_ROWS = SUBLANES
F32 = jnp.float32
BF16 = jnp.bfloat16


def dft_table(win):
    line = np.arange(win, dtype=np.int64)
    angle = (line[:, None] * line[None, :] % win) * (2.0 * np.pi / win)
    full = (np.stack([np.cos(angle), np.sin(angle)]) / np.sqrt(win)).astype(np.float32)
    high = full.astype(jnp.bfloat16)
    low = (full - high.astype(np.float32)).astype(jnp.bfloat16)
    return np.concatenate([high, low])


def pairings(size):
    found = []
    for first in (0, 1):
        pairs = {}
        for low in range(first, size - 1, 2):
            pairs[low], pairs[low + 1] = low + 1, low
        if pairs:
            found.append(pairs)
    return found


def flat_pairs(pairs_y, pairs_x, n_ty, n_tx):
    out, alone = [], []
    for x in range(n_tx):
        for y in range(n_ty):
            to_y = y if pairs_y is None else pairs_y.get(y)
            to_x = x if pairs_x is None else pairs_x.get(x)
            if to_y is None or to_x is None:
                alone.append(y * n_tx + x)
            else:
                out.append((y * n_tx + x, to_y * n_tx + to_x))
    for a, b in zip(alone[::2], alone[1::2]):
        out += [(a, b), (b, a)]
    if len(alone) % 2:
        out.append((alone[-1], alone[-1]))
    return out


def if_paired(x, at, size, i):
    last = i + 2 * ((size - i) // 2)
    if i > 0:
        x = jnp.where(at >= i, x, 0.0)
    return jnp.where(at < last, x, 0.0) if last < size else x


def xor_permute(x, mask, total):
    return lax.ppermute(x, AXES, [(i, i ^ mask) for i in range(total)])


def split(x):
    high = x.astype(BF16)
    return high, (x - high.astype(F32)).astype(BF16)


def product(a, b):
    (a_high, a_low), (b_high, b_low) = a, b
    return jnp.dot(
        jnp.concatenate([a_high, a_low, a_high], axis=1),
        jnp.concatenate([b_high, b_high, b_low], axis=0),
        preferred_element_type=F32,
    )


def block(c, upper, lower):
    return jnp.concatenate(
        [jnp.concatenate([c, upper], axis=1), jnp.concatenate([lower, c], axis=1)], axis=0
    )


def lane_pick(width, margin, flag):
    lane = lax.broadcasted_iota(jnp.int32, (8, width), 1)
    below = jnp.where(lane < margin, 0, 1)
    return below == flag


def rowwise(mask, rows):
    return jnp.broadcast_to(mask[:1], (rows, mask.shape[1]))


def by_parity(odd, even_value, odd_value):
    return jnp.where(odd == 1, odd_value, even_value)


def compute(
    ext_ref, probe_ref, root_ref, pos_ref, table_ref, grid_ref, grad_ref, *, margin
):
    scans, win = root_ref.shape[0], root_ref.shape[1]
    modes = probe_ref.shape[1]
    width = 2 * win
    w_fwd = [block(table_ref[i], -table_ref[i + 1], table_ref[i + 1]) for i in (0, 2)]
    l_fwd = [block(table_ref[i], table_ref[i + 1], -table_ref[i + 1]) for i in (0, 2)]
    grid_ref[...] = jnp.zeros_like(grid_ref)
    weight = jnp.zeros((WEIGHT_ROWS, win), F32)
    for s in range(scans):
        r, c = pos_ref[s, 0], pos_ref[s, 1]
        turn = jnp.where(c <= margin, margin - c, margin + width - c)
        back = jnp.where(c >= margin, c - margin, c + width - margin)
        q = r % SUBLANES
        base = pl.multiple_of(r - q, SUBLANES)
        tall = win + SUBLANES
        lift = jnp.where(q == 0, 0, tall - q)

        def window(part):
            band = pltpu.roll(ext_ref[part, pl.ds(base, tall), :], turn, 1)[:, :win]
            return pltpu.roll(band, lift, 0)[:win]

        o_re, o_im = window(0), window(1)
        power = o_re * o_re + o_im * o_im
        weight = weight + jnp.sum(power.reshape(win // WEIGHT_ROWS, WEIGHT_ROWS, win), axis=0)
        rows = []
        for k in range(modes):
            p_re, p_im = probe_ref[0, k], probe_ref[1, k]
            rows.append(
                jnp.concatenate([p_re * o_re - p_im * o_im, p_re * o_im + p_im * o_re], axis=1)
            )
        y = product(split(jnp.concatenate(rows, axis=0)), w_fwd)
        y = jnp.concatenate(
            [
                jnp.concatenate([y[k * win : (k + 1) * win, :win] for k in range(modes)], axis=1),
                jnp.concatenate([y[k * win : (k + 1) * win, win:] for k in range(modes)], axis=1),
            ],
            axis=0,
        )
        far = product(l_fwd, split(y))
        square = far * far
        square = square[:win] + square[win:]
        total = square[:, :win]
        for k in range(1, modes):
            total = total + square[:, k * win : (k + 1) * win]
        ratio = root_ref[s] * lax.rsqrt(jnp.maximum(total, 1.0)) - 1.0
        ratio = jnp.concatenate([ratio] * modes, axis=1)
        far = far * jnp.concatenate([ratio, ratio], axis=0)
        u = product(w_fwd, split(far))
        u = jnp.concatenate(
            [
                jnp.concatenate(
                    [u[:win, k * win : (k + 1) * win], u[win:, k * win : (k + 1) * win]], axis=1
                )
                for k in range(modes)
            ],
            axis=0,
        )
        chi = product(split(u), l_fwd)
        g_re = g_im = None
        for k in range(modes):
            p_re, p_im = probe_ref[0, k], probe_ref[1, k]
            c_re, c_im = chi[k * win : (k + 1) * win, :win], chi[k * win : (k + 1) * win, win:]
            a, b = p_re * c_re + p_im * c_im, p_re * c_im - p_im * c_re
            g_re, g_im = (a, b) if k == 0 else (g_re + a, g_im + b)
            a, b = o_re * c_re + o_im * c_im, o_re * c_im - o_im * c_re
            if s == 0:
                grad_ref[k], grad_ref[modes + k] = a, b
            else:
                grad_ref[k] += a
                grad_ref[modes + k] += b
        for part, g in ((0, g_re), (1, g_im)):
            g = pltpu.roll(jnp.concatenate([g, jnp.zeros((SUBLANES, win), F32)], axis=0), q, 0)
            g = jnp.concatenate([g, jnp.zeros_like(g)], axis=1)
            grid_ref[part, pl.ds(base, tall), :] += pltpu.roll(g, back, 1)
    return weight


def emit(grad_ref, weight, grid_ref, keep_ref, send_ref, first_ref, second_ref, rim_refs, margin):
    count, win = keep_ref.shape[0], grad_ref.shape[1]
    odd_y, odd_x = lax.axis_index("ty") % 2, lax.axis_index("tx") % 2
    for j in range(count):
        keep_ref[j, :win, :] = grad_ref[odd_x * count + j]
        send_ref[j, :win, :] = grad_ref[(1 - odd_x) * count + j]
        keep_ref[j, win:, :] = weight
        send_ref[j, win:, :] = weight
    tile = first_ref.shape[-1]
    mask = rowwise(lane_pick(tile, margin, odd_x), tile)
    for part in (0, 1):
        rows = grid_ref[part, margin : margin + tile, :]
        first_ref[part], second_ref[part] = chosen(mask, rows[:, tile:], rows[:, :tile])
        for i, ref in enumerate(rim_refs):
            start = pl.multiple_of(jnp.where(odd_y == i, 2 * tile - margin, 0), margin)
            rows = grid_ref[part, pl.ds(start, margin), :]
            ref[0, part], ref[1, part] = chosen(mask[:margin], rows[:, tile:], rows[:, :tile])


def chosen(mask, a, b):
    return jnp.where(mask, a, b), jnp.where(mask, b, a)


def prepare_kernel(probe_ref, meas_ref, table_ref, probe_out, root_ref, table_out):
    probe_out[...] = probe_ref[...]
    root_ref[...] = jnp.sqrt(meas_ref[...])
    table_out[...] = table_ref[...]


def first_kernel(n_ty, n_tx, n_y, n_x, margin, pos_ref, obj_ref, probe_ref, root_ref, table_ref, *rest):
    take = iter(rest)
    ty_refs = [next(take) for _ in range(n_y)]
    tx_refs = [next(take) for _ in range(n_x)]
    corner_refs = [[next(take) for _ in range(n_x)] for _ in range(n_y)]
    ext_ref, keep_ref, send_ref, first_ref, second_ref, *rim_refs = take
    *rim_refs, grid_ref, grad_ref = rim_refs
    tile = obj_ref.shape[-1]
    at_y, at_x = lax.axis_index("ty"), lax.axis_index("tx")
    odd_y, odd_x = at_y % 2, at_x % 2
    pick = lane_pick(tile, margin, odd_x)

    def side(refs, part, rows):
        both = [if_paired(ref[part], at_x, n_tx, i) for i, ref in enumerate(refs)]
        both += [jnp.zeros((rows, tile), F32)] * (2 - n_x)
        return jnp.where(rowwise(pick, rows), both[0], both[1])

    for part in (0, 1):
        ext_ref[part, margin : margin + tile, :tile] = obj_ref[part]
        ext_ref[part, margin : margin + tile, tile:] = side(tx_refs, part, tile)
        bands = [
            if_paired(
                jnp.concatenate([ty_refs[i][part], side(corner_refs[i], part, margin)], axis=1),
                at_y, n_ty, i,
            )
            for i in range(n_y)
        ]
        bands += [jnp.zeros((margin, 2 * tile), F32)] * (2 - n_y)
        ext_ref[part, :margin, :] = by_parity(odd_y, bands[1], bands[0])
        ext_ref[part, margin + tile : 2 * tile, :] = by_parity(odd_y, bands[0], bands[1])
    weight = compute(
        ext_ref, probe_ref, root_ref, pos_ref, table_ref, grid_ref, grad_ref, margin=margin
    )
    emit(
        grad_ref, weight, grid_ref, keep_ref, send_ref, first_ref, second_ref, rim_refs, margin
    )


def combined_probe(probe_ref, own_ref, other_ref, new_ref, half):
    count, win, modes = own_ref.shape[0], probe_ref.shape[-1], probe_ref.shape[1]
    weight = jnp.sum(own_ref[0, win:, :])
    scale = PROBE_RELAX * win * win / jnp.full((8, win), weight, F32)
    scale = jnp.broadcast_to(scale[:1], (win, win))
    for j in range(count):
        for ref, index in ((own_ref, half * count + j), (other_ref, (1 - half) * count + j)):
            part, k = index // modes, index % modes
            new_ref[part, k] = probe_ref[part, k] + scale * ref[j, :win, :]


def second_kernel(
    n_ty, n_tx, n_y, n_x, margin, pos_ref, old_ref, first_ref, second_ref, probe_ref, root_ref,
    table_ref, own_ref, other_ref, *rest
):
    take = iter(rest)
    tx_refs = [next(take) for _ in range(n_x)]
    halo_refs = [next(take) for _ in range(n_y)]
    tile_ref, new_ref, keep_ref, send_ref, next_first_ref, next_second_ref, *rim_refs = take
    *rim_refs, ext_ref, grid_ref, grad_ref = rim_refs
    tile = probe_ref.shape[-1]
    at_y, at_x = lax.axis_index("ty"), lax.axis_index("tx")
    odd_y, odd_x = at_y % 2, at_x % 2
    combined_probe(probe_ref, own_ref, other_ref, new_ref, odd_x)
    row = lax.broadcasted_iota(jnp.int32, (2 * tile, 2 * tile), 0)
    lane = lax.broadcasted_iota(jnp.int32, (2 * tile, 2 * tile), 1)
    inside = (row >= jnp.where(at_y == 0, margin, 0)) & (
        row < jnp.where(at_y == n_ty - 1, margin + tile, 2 * tile)
    )
    inside &= (lane < jnp.where(at_x == n_tx - 1, tile, tile + margin)) | (
        lane >= jnp.where(at_x == 0, 2 * tile, tile + margin)
    )
    mask = rowwise(lane_pick(tile, margin, odd_x), tile)
    for i in range(2):
        start = pl.multiple_of(jnp.where(odd_y == i, margin + tile, 0), margin)
        for part in (0, 1):
            if i < n_y:
                ref = halo_refs[i]
                own, margins = chosen(mask[:margin], ref[1, part], ref[0, part])
                rows = jnp.concatenate([own, margins], axis=1)
            else:
                rows = jnp.zeros((margin, 2 * tile), F32)
            ext_ref[part, pl.ds(start, margin), :] = rows
    for part in (0, 1):
        both = [first_ref[part], second_ref[part]]
        for i, ref in enumerate(tx_refs):
            both[i] = both[i] + if_paired(ref[part], at_x, n_tx, i)
        own, margins = chosen(mask, both[1], both[0])
        ext_ref[part, margin : margin + tile, :] = jnp.concatenate([own, margins], axis=1)
        step = jnp.where(inside, OBJECT_STEP * ext_ref[part, : 2 * tile, :], 0.0)
        ext_ref[part, : 2 * tile, :] = old_ref[part, : 2 * tile, :] + step
        tile_ref[part] = ext_ref[part, margin : margin + tile, :tile]
    weight = compute(
        ext_ref, new_ref, root_ref, pos_ref, table_ref, grid_ref, grad_ref, margin=margin
    )
    emit(
        grad_ref, weight, grid_ref, keep_ref, send_ref, next_first_ref, next_second_ref, rim_refs,
        margin,
    )


def last_kernel(
    n_tx, n_x, margin, tile_ref, first_ref, second_ref, probe_ref, own_ref, other_ref, *rest
):
    *tx_refs, obj_ref, new_ref = rest
    tile = tile_ref.shape[-1]
    at_x = lax.axis_index("tx")
    combined_probe(probe_ref, own_ref, other_ref, new_ref, at_x % 2)
    mask = rowwise(lane_pick(tile, margin, at_x % 2), tile)
    for part in (0, 1):
        both = [first_ref[part], second_ref[part]]
        for i, ref in enumerate(tx_refs):
            both[i] = both[i] + if_paired(ref[part], at_x, n_tx, i)
        obj_ref[part] = tile_ref[part] + OBJECT_STEP * chosen(mask, both[1], both[0])[0]


def call(kernel, outs, ins, scratch=()):
    smem = pl.BlockSpec(memory_space=pltpu.SMEM)
    vmem = pl.BlockSpec(memory_space=pltpu.VMEM)
    shapes = [s if hasattr(s, "dtype") else jax.ShapeDtypeStruct(s, F32) for s in outs]
    return pl.pallas_call(
        kernel,
        out_shape=shapes,
        in_specs=[smem if x.dtype == jnp.int32 else vmem for x in ins],
        out_specs=[vmem] * len(outs),
        scratch_shapes=[pltpu.VMEM(s, F32) for s in scratch],
        compiler_params=pltpu.CompilerParams(vmem_limit_bytes=16 * 1024 * 1024),
    )(*ins)


def bit_of(me, bit):
    return (me >> bit) & 1


def masks_of(bits):
    return [sum(((m >> i) & 1) << b for i, b in enumerate(bits)) for m in range(1, 1 << len(bits))]


def local_index(me, bits):
    return sum(bit_of(me, b) << i for i, b in enumerate(bits))


def tree(values):
    while len(values) > 1:
        values = [a + b for a, b in zip(values[::2], values[1::2])] + values[len(values) & ~1 :]
    return values[0]


def scatter_sum(x, me, bits, total):
    here = local_index(me, bits)
    n = 1 << len(bits)
    x = x.reshape((n, x.shape[0] // n) + x.shape[1:])
    parts = [lax.dynamic_index_in_dim(x, here, 0, False)]
    for m, mask in enumerate(masks_of(bits), 1):
        parts.append(xor_permute(lax.dynamic_index_in_dim(x, here ^ m, 0, False), mask, total))
    return tree(parts)


def direct_sum(x, bits, total):
    return tree([x] + [xor_permute(x, mask, total) for mask in masks_of(bits)])


def gather(x, me, bits, total):
    here = local_index(me, bits)
    parts = jnp.stack([x] + [xor_permute(x, mask, total) for mask in masks_of(bits)])
    return jnp.concatenate(
        [lax.dynamic_index_in_dim(parts, here ^ j, 0, False) for j in range(1 << len(bits))]
    )


def summed_halves(keep, send, n_ty, n_tx, steps):
    total = n_ty * n_tx
    me = lax.axis_index("ty") * n_tx + lax.axis_index("tx")
    levels = total.bit_length() - 1
    tx_bits = n_tx.bit_length() - 1
    bits = [b for b in (tx_bits, 1) if b < levels]
    rest = [b for b in range(1, levels) if b not in bits]
    half = keep + xor_permute(send, 1, total)
    done = [steps[0]()]
    half = scatter_sum(half, me, bits, total)
    half, done[0] = lax.optimization_barrier((half, done[0]))
    done.append(steps[1](*done))
    for i in range(0, len(rest), 2):
        half = direct_sum(half, rest[i : i + 2], total)
    half, done[1] = lax.optimization_barrier((half, done[1]))
    done += [step(*done) for step in steps[2:]]
    half = gather(half, me, bits, total)
    if steps[2:]:
        half, done[2] = lax.optimization_barrier((half, done[2]))
    return half, xor_permute(half, 1, total), done


def per_device(n_ty, n_tx, table, object_field, probe, intensities, positions):
    win, modes = probe.shape[-1], probe.shape[1]
    margin, tile, scans = win // 2, object_field.shape[-1], positions.shape[2]
    spots = positions.reshape(scans, 2)
    measured = intensities.reshape(scans, win, win)
    match_y, match_x = pairings(n_ty), pairings(n_tx)
    n_y, n_x = len(match_y), len(match_x)
    odd_y = lax.axis_index("ty") % 2

    def swap(x, pairs_y, pairs_x):
        return lax.ppermute(x, AXES, flat_pairs(pairs_y, pairs_x, n_ty, n_tx))

    def rows_for(x, i, count, low, high):
        start = jnp.where(odd_y == i, high, low)
        return lax.dynamic_slice_in_dim(x, start, count, 1)

    tx_in = [swap(object_field, None, px) for px in match_x]
    rims = [rows_for(object_field, i, margin, 0, tile - margin) for i in range(n_y)]
    ty_in = [swap(rims[i], py, None) for i, py in enumerate(match_y)]
    corners = []
    for i, py in enumerate(match_y):
        corners += [swap(ty_in[i], None, px) for px in match_x[:1]]
        corners += [swap(rims[i], py, px) for px in match_x[1:]]

    shape_of = lambda x: jax.ShapeDtypeStruct(x.shape, x.dtype)
    ready = (probe, measured, jnp.asarray(table))
    ready = call(prepare_kernel, [shape_of(x) for x in ready], ready)
    (tx_in, ty_in, corners), (probe, root, table) = lax.optimization_barrier(
        ((tx_in, ty_in, corners), tuple(ready))
    )

    at_y, at_x = lax.axis_index("ty"), lax.axis_index("tx")
    half_shape = (modes, win + WEIGHT_ROWS, win)
    grid_shape = (2, 2 * tile + SUBLANES, 2 * tile)
    sent = [half_shape] * 2 + [object_field.shape] * 2 + [(2, 2, margin, tile)] * n_y
    scratch = [grid_shape, (2 * modes, win, win)]

    def exchanges(overlaps, rims):
        def folded(received):
            halves = [x.reshape(2, 2, margin, tile) for x in overlaps]
            place = lax.broadcasted_iota(jnp.int32, (1, 2, 1, 1), 1)
            for i, y in enumerate(received):
                here = place == jnp.where(odd_y == i, 1, 0)
                for k in (0, 1):
                    extra = if_paired(y[k][:, None], at_y, n_ty, i)
                    halves[k] = halves[k] + jnp.where(here, extra, 0.0)
            return [x.reshape(object_field.shape) for x in halves]

        def fold():
            return [swap(rim, py, None) for rim, py in zip(rims, match_y)]

        def across(received):
            mine = folded(received)
            return mine, [swap(x, None, px) for x, px in zip(mine, match_x)]

        def halo(received, columns):
            mine, theirs = columns
            total = list(mine)
            for i, x in enumerate(theirs):
                total[i] = total[i] + if_paired(x, at_x, n_tx, i)
            bands = [
                jnp.stack([rows_for(x, i, margin, 0, tile - margin) for x in total])
                for i in range(n_y)
            ]
            return [swap(band, py, None) for band, py in zip(bands, match_y)]

        return fold, across, halo

    ext, keep, send, first, second, *rims = call(
        functools.partial(first_kernel, n_ty, n_tx, n_y, n_x, margin),
        [grid_shape] + sent,
        [spots, object_field, probe, root, table, *ty_in, *tx_in, *corners],
        scratch,
    )
    steps = exchanges([first, second], rims)
    own, other, (_, (overlaps, tx_in), halo) = summed_halves(keep, send, n_ty, n_tx, steps)
    tile_mid, probe_mid, keep, send, first, second, *rims = call(
        functools.partial(second_kernel, n_ty, n_tx, n_y, n_x, margin),
        [object_field.shape, probe.shape] + sent,
        [spots, ext, *overlaps, probe, root, table, own, other, *tx_in, *halo],
        [grid_shape] + scratch,
    )
    steps = exchanges([first, second], rims)
    own, other, (_, (overlaps, tx_in)) = summed_halves(keep, send, n_ty, n_tx, steps[:2])
    return call(
        functools.partial(last_kernel, n_tx, n_x, margin),
        [object_field.shape, probe.shape],
        [tile_mid, *overlaps, probe_mid, own, other, *tx_in],
    )


def solution(mesh):
    n_ty, n_tx = mesh.shape["ty"], mesh.shape["tx"]
    placed = (P(None, "ty", "tx"), P(), P("ty", "tx", None, None, None), P("ty", "tx", None, None))

    def run(object_field, probe, intensities, positions):
        table = dft_table(probe.shape[-1])
        return jax.shard_map(
            functools.partial(per_device, n_ty, n_tx, table),
            mesh=mesh,
            in_specs=placed,
            out_specs=(P(None, "ty", "tx"), P()),
            check_vma=False,
        )(object_field, probe, intensities, positions)

    return run
```

```python
import functools

import jax
import jax.numpy as jnp
import numpy as np
from jax import lax
from jax.experimental import pallas as pl
from jax.experimental.pallas import tpu as pltpu
from jax.sharding import PartitionSpec as P

ROUNDS = 2
OBJECT_STEP = 0.1
PROBE_RELAX = 0.5
AXES = ("ty", "tx")
SUBLANES = 8
WEIGHT_ROWS = SUBLANES
F32 = jnp.float32
BF16 = jnp.bfloat16


def dft_table(win):
    line = np.arange(win, dtype=np.int64)
    angle = (line[:, None] * line[None, :] % win) * (2.0 * np.pi / win)
    full = (np.stack([np.cos(angle), np.sin(angle)]) / np.sqrt(win)).astype(np.float32)
    high = full.astype(jnp.bfloat16)
    low = (full - high.astype(np.float32)).astype(jnp.bfloat16)
    return np.concatenate([high, low])


def pairings(size):
    found = []
    for first in (0, 1):
        pairs = {}
        for low in range(first, size - 1, 2):
            pairs[low], pairs[low + 1] = low + 1, low
        if pairs:
            found.append(pairs)
    return found


def flat_pairs(pairs_y, pairs_x, n_ty, n_tx):
    out, alone = [], []
    for x in range(n_tx):
        for y in range(n_ty):
            to_y = y if pairs_y is None else pairs_y.get(y)
            to_x = x if pairs_x is None else pairs_x.get(x)
            if to_y is None or to_x is None:
                alone.append(y * n_tx + x)
            else:
                out.append((y * n_tx + x, to_y * n_tx + to_x))
    for a, b in zip(alone[::2], alone[1::2]):
        out += [(a, b), (b, a)]
    if len(alone) % 2:
        out.append((alone[-1], alone[-1]))
    return out


def if_paired(x, at, size, i):
    last = i + 2 * ((size - i) // 2)
    if i > 0:
        x = jnp.where(at >= i, x, 0.0)
    return jnp.where(at < last, x, 0.0) if last < size else x


def xor_permute(x, mask, total):
    return lax.ppermute(x, AXES, [(i, i ^ mask) for i in range(total)])


def split(x):
    high = x.astype(BF16)
    return high, (x - high.astype(F32)).astype(BF16)


def product(a, b):
    (a_high, a_low), (b_high, b_low) = a, b
    return jnp.dot(
        jnp.concatenate([a_high, a_low, a_high], axis=1),
        jnp.concatenate([b_high, b_high, b_low], axis=0),
        preferred_element_type=F32,
    )


def block(c, upper, lower):
    return jnp.concatenate(
        [jnp.concatenate([c, upper], axis=1), jnp.concatenate([lower, c], axis=1)], axis=0
    )


def lane_pick(width, margin, flag):
    lane = lax.broadcasted_iota(jnp.int32, (8, width), 1)
    below = jnp.where(lane < margin, 0, 1)
    return below == flag


def rowwise(mask, rows):
    return jnp.broadcast_to(mask[:1], (rows, mask.shape[1]))


def by_parity(odd, even_value, odd_value):
    return jnp.where(odd == 1, odd_value, even_value)


def compute(
    ext_ref, probe_ref, root_ref, pos_ref, table_ref, grid_ref, grad_ref, *, margin
):
    scans, win = root_ref.shape[0], root_ref.shape[1]
    modes = probe_ref.shape[1]
    width, tall = 2 * win, win + SUBLANES
    w_fwd = [block(table_ref[i], -table_ref[i + 1], table_ref[i + 1]) for i in (0, 2)]
    l_fwd = [block(table_ref[i], table_ref[i + 1], -table_ref[i + 1]) for i in (0, 2)]
    grid_ref[...] = jnp.zeros_like(grid_ref)
    windows, state, weights = {}, {}, []

    def corner(s):
        r, c = pos_ref[s, 0], pos_ref[s, 1]
        q = r % SUBLANES
        return pl.multiple_of(r - q, SUBLANES), q, c

    def enter(s):
        base, q, c = corner(s)
        turn = jnp.where(c <= margin, margin - c, margin + width - c)
        lift = jnp.where(q == 0, 0, tall - q)

        def window(part):
            band = pltpu.roll(ext_ref[part, pl.ds(base, tall), :], turn, 1)[:, :win]
            return pltpu.roll(band, lift, 0)[:win]

        o_re, o_im = windows[s] = window(0), window(1)
        power = o_re * o_re + o_im * o_im
        weights.append(jnp.sum(power.reshape(win // WEIGHT_ROWS, WEIGHT_ROWS, win), axis=0))
        rows = []
        for k in range(modes):
            p_re, p_im = probe_ref[0, k], probe_ref[1, k]
            rows.append(
                jnp.concatenate([p_re * o_re - p_im * o_im, p_re * o_im + p_im * o_re], axis=1)
            )
        state[s] = product(split(jnp.concatenate(rows, axis=0)), w_fwd)

    def forward(s):
        y = state[s]
        y = jnp.concatenate(
            [
                jnp.concatenate([y[k * win : (k + 1) * win, :win] for k in range(modes)], axis=1),
                jnp.concatenate([y[k * win : (k + 1) * win, win:] for k in range(modes)], axis=1),
            ],
            axis=0,
        )
        state[s] = product(l_fwd, split(y))

    def scale(s):
        far = state[s]
        square = far * far
        square = square[:win] + square[win:]
        total = square[:, :win]
        for k in range(1, modes):
            total = total + square[:, k * win : (k + 1) * win]
        ratio = root_ref[s] * lax.rsqrt(jnp.maximum(total, 1.0)) - 1.0
        ratio = jnp.concatenate([ratio] * modes, axis=1)
        far = far * jnp.concatenate([ratio, ratio], axis=0)
        state[s] = product(w_fwd, split(far))

    def backward(s):
        u = state[s]
        u = jnp.concatenate(
            [
                jnp.concatenate(
                    [u[:win, k * win : (k + 1) * win], u[win:, k * win : (k + 1) * win]], axis=1
                )
                for k in range(modes)
            ],
            axis=0,
        )
        state[s] = product(split(u), l_fwd)

    def leave(s):
        chi = state[s]
        o_re, o_im = windows[s]
        g_re = g_im = None
        for k in range(modes):
            p_re, p_im = probe_ref[0, k], probe_ref[1, k]
            c_re, c_im = chi[k * win : (k + 1) * win, :win], chi[k * win : (k + 1) * win, win:]
            a, b = p_re * c_re + p_im * c_im, p_re * c_im - p_im * c_re
            g_re, g_im = (a, b) if k == 0 else (g_re + a, g_im + b)
            a, b = o_re * c_re + o_im * c_im, o_re * c_im - o_im * c_re
            if s == 0:
                grad_ref[k], grad_ref[modes + k] = a, b
            else:
                grad_ref[k] += a
                grad_ref[modes + k] += b
        base, q, c = corner(s)
        back = jnp.where(c >= margin, c - margin, c + width - margin)
        for part, g in ((0, g_re), (1, g_im)):
            g = pltpu.roll(jnp.concatenate([g, jnp.zeros((SUBLANES, win), F32)], axis=0), q, 0)
            g = jnp.concatenate([g, jnp.zeros_like(g)], axis=1)
            grid_ref[part, pl.ds(base, tall), :] += pltpu.roll(g, back, 1)

    stages = (enter, forward, scale, backward, leave)
    for stage in stages:
        for s in range(scans):
            stage(s)
    return functools.reduce(jnp.add, weights)


def emit(grad_ref, weight, grid_ref, keep_ref, send_ref, first_ref, second_ref, rim_refs, margin):
    count, win = keep_ref.shape[0], grad_ref.shape[1]
    odd_y, odd_x = lax.axis_index("ty") % 2, lax.axis_index("tx") % 2
    for j in range(count):
        keep_ref[j, :win, :] = grad_ref[odd_x * count + j]
        send_ref[j, :win, :] = grad_ref[(1 - odd_x) * count + j]
        keep_ref[j, win:, :] = weight
        send_ref[j, win:, :] = weight
    tile = first_ref.shape[-1]
    mask = rowwise(lane_pick(tile, margin, odd_x), tile)
    for part in (0, 1):
        rows = grid_ref[part, margin : margin + tile, :]
        first_ref[part], second_ref[part] = chosen(mask, rows[:, tile:], rows[:, :tile])
        for i, ref in enumerate(rim_refs):
            start = pl.multiple_of(jnp.where(odd_y == i, 2 * tile - margin, 0), margin)
            rows = grid_ref[part, pl.ds(start, margin), :]
            ref[0, part], ref[1, part] = chosen(mask[:margin], rows[:, tile:], rows[:, :tile])


def chosen(mask, a, b):
    return jnp.where(mask, a, b), jnp.where(mask, b, a)


def prepare_kernel(probe_ref, meas_ref, table_ref, probe_out, root_ref, table_out):
    probe_out[...] = probe_ref[...]
    root_ref[...] = jnp.sqrt(meas_ref[...])
    table_out[...] = table_ref[...]


def first_kernel(n_ty, n_tx, n_y, n_x, margin, pos_ref, obj_ref, probe_ref, root_ref, table_ref, *rest):
    take = iter(rest)
    ty_refs = [next(take) for _ in range(n_y)]
    tx_refs = [next(take) for _ in range(n_x)]
    corner_refs = [[next(take) for _ in range(n_x)] for _ in range(n_y)]
    ext_ref, keep_ref, send_ref, first_ref, second_ref, *rim_refs = take
    *rim_refs, grid_ref, grad_ref = rim_refs
    tile = obj_ref.shape[-1]
    at_y, at_x = lax.axis_index("ty"), lax.axis_index("tx")
    odd_y, odd_x = at_y % 2, at_x % 2
    pick = lane_pick(tile, margin, odd_x)

    def side(refs, part, rows):
        both = [if_paired(ref[part], at_x, n_tx, i) for i, ref in enumerate(refs)]
        both += [jnp.zeros((rows, tile), F32)] * (2 - n_x)
        return jnp.where(rowwise(pick, rows), both[0], both[1])

    for part in (0, 1):
        ext_ref[part, margin : margin + tile, :tile] = obj_ref[part]
        ext_ref[part, margin : margin + tile, tile:] = side(tx_refs, part, tile)
        bands = [
            if_paired(
                jnp.concatenate([ty_refs[i][part], side(corner_refs[i], part, margin)], axis=1),
                at_y, n_ty, i,
            )
            for i in range(n_y)
        ]
        bands += [jnp.zeros((margin, 2 * tile), F32)] * (2 - n_y)
        ext_ref[part, :margin, :] = by_parity(odd_y, bands[1], bands[0])
        ext_ref[part, margin + tile : 2 * tile, :] = by_parity(odd_y, bands[0], bands[1])
    weight = compute(
        ext_ref, probe_ref, root_ref, pos_ref, table_ref, grid_ref, grad_ref, margin=margin
    )
    emit(
        grad_ref, weight, grid_ref, keep_ref, send_ref, first_ref, second_ref, rim_refs, margin
    )


def combined_probe(probe_ref, own_ref, other_ref, new_ref, half):
    count, win, modes = own_ref.shape[0], probe_ref.shape[-1], probe_ref.shape[1]
    weight = jnp.sum(own_ref[0, win:, :])
    scale = PROBE_RELAX * win * win / jnp.full((8, win), weight, F32)
    scale = jnp.broadcast_to(scale[:1], (win, win))
    for j in range(count):
        for ref, index in ((own_ref, half * count + j), (other_ref, (1 - half) * count + j)):
            part, k = index // modes, index % modes
            new_ref[part, k] = probe_ref[part, k] + scale * ref[j, :win, :]


def second_kernel(
    n_ty, n_tx, n_y, n_x, margin, pos_ref, old_ref, first_ref, second_ref, probe_ref, root_ref,
    table_ref, own_ref, other_ref, *rest
):
    take = iter(rest)
    tx_refs = [next(take) for _ in range(n_x)]
    halo_refs = [next(take) for _ in range(n_y)]
    tile_ref, new_ref, keep_ref, send_ref, next_first_ref, next_second_ref, *rim_refs = take
    *rim_refs, ext_ref, grid_ref, grad_ref = rim_refs
    tile = probe_ref.shape[-1]
    at_y, at_x = lax.axis_index("ty"), lax.axis_index("tx")
    odd_y, odd_x = at_y % 2, at_x % 2
    combined_probe(probe_ref, own_ref, other_ref, new_ref, odd_x)
    row = lax.broadcasted_iota(jnp.int32, (2 * tile, 2 * tile), 0)
    lane = lax.broadcasted_iota(jnp.int32, (2 * tile, 2 * tile), 1)
    inside = (row >= jnp.where(at_y == 0, margin, 0)) & (
        row < jnp.where(at_y == n_ty - 1, margin + tile, 2 * tile)
    )
    inside &= (lane < jnp.where(at_x == n_tx - 1, tile, tile + margin)) | (
        lane >= jnp.where(at_x == 0, 2 * tile, tile + margin)
    )
    mask = rowwise(lane_pick(tile, margin, odd_x), tile)
    for i in range(2):
        start = pl.multiple_of(jnp.where(odd_y == i, margin + tile, 0), margin)
        for part in (0, 1):
            if i < n_y:
                ref = halo_refs[i]
                own, margins = chosen(mask[:margin], ref[1, part], ref[0, part])
                rows = jnp.concatenate([own, margins], axis=1)
            else:
                rows = jnp.zeros((margin, 2 * tile), F32)
            ext_ref[part, pl.ds(start, margin), :] = rows
    for part in (0, 1):
        both = [first_ref[part], second_ref[part]]
        for i, ref in enumerate(tx_refs):
            both[i] = both[i] + if_paired(ref[part], at_x, n_tx, i)
        own, margins = chosen(mask, both[1], both[0])
        ext_ref[part, margin : margin + tile, :] = jnp.concatenate([own, margins], axis=1)
        step = jnp.where(inside, OBJECT_STEP * ext_ref[part, : 2 * tile, :], 0.0)
        ext_ref[part, : 2 * tile, :] = old_ref[part, : 2 * tile, :] + step
        tile_ref[part] = ext_ref[part, margin : margin + tile, :tile]
    weight = compute(
        ext_ref, new_ref, root_ref, pos_ref, table_ref, grid_ref, grad_ref, margin=margin
    )
    emit(
        grad_ref, weight, grid_ref, keep_ref, send_ref, next_first_ref, next_second_ref, rim_refs,
        margin,
    )


def last_kernel(
    n_tx, n_x, margin, tile_ref, first_ref, second_ref, probe_ref, own_ref, other_ref, *rest
):
    *tx_refs, obj_ref, new_ref = rest
    tile = tile_ref.shape[-1]
    at_x = lax.axis_index("tx")
    combined_probe(probe_ref, own_ref, other_ref, new_ref, at_x % 2)
    mask = rowwise(lane_pick(tile, margin, at_x % 2), tile)
    for part in (0, 1):
        both = [first_ref[part], second_ref[part]]
        for i, ref in enumerate(tx_refs):
            both[i] = both[i] + if_paired(ref[part], at_x, n_tx, i)
        obj_ref[part] = tile_ref[part] + OBJECT_STEP * chosen(mask, both[1], both[0])[0]


def call(kernel, outs, ins, scratch=()):
    smem = pl.BlockSpec(memory_space=pltpu.SMEM)
    vmem = pl.BlockSpec(memory_space=pltpu.VMEM)
    shapes = [s if hasattr(s, "dtype") else jax.ShapeDtypeStruct(s, F32) for s in outs]
    return pl.pallas_call(
        kernel,
        out_shape=shapes,
        in_specs=[smem if x.dtype == jnp.int32 else vmem for x in ins],
        out_specs=[vmem] * len(outs),
        scratch_shapes=[pltpu.VMEM(s, F32) for s in scratch],
        compiler_params=pltpu.CompilerParams(vmem_limit_bytes=16 * 1024 * 1024),
    )(*ins)


def bit_of(me, bit):
    return (me >> bit) & 1


def masks_of(bits):
    return [sum(((m >> i) & 1) << b for i, b in enumerate(bits)) for m in range(1, 1 << len(bits))]


def local_index(me, bits):
    return sum(bit_of(me, b) << i for i, b in enumerate(bits))


def tree(values):
    while len(values) > 1:
        values = [a + b for a, b in zip(values[::2], values[1::2])] + values[len(values) & ~1 :]
    return values[0]


def scatter_sum(x, me, bits, total):
    here = local_index(me, bits)
    n = 1 << len(bits)
    x = x.reshape((n, x.shape[0] // n) + x.shape[1:])
    parts = [lax.dynamic_index_in_dim(x, here, 0, False)]
    for m, mask in enumerate(masks_of(bits), 1):
        parts.append(xor_permute(lax.dynamic_index_in_dim(x, here ^ m, 0, False), mask, total))
    return tree(parts)


def direct_sum(x, bits, total):
    return tree([x] + [xor_permute(x, mask, total) for mask in masks_of(bits)])


def gather(x, me, bits, total):
    here = local_index(me, bits)
    parts = jnp.stack([x] + [xor_permute(x, mask, total) for mask in masks_of(bits)])
    return jnp.concatenate(
        [lax.dynamic_index_in_dim(parts, here ^ j, 0, False) for j in range(1 << len(bits))]
    )


def summed_halves(keep, send, n_ty, n_tx, steps):
    total = n_ty * n_tx
    me = lax.axis_index("ty") * n_tx + lax.axis_index("tx")
    levels = total.bit_length() - 1
    tx_bits = n_tx.bit_length() - 1
    bits = [b for b in (tx_bits, 1) if b < levels]
    rest = [b for b in range(1, levels) if b not in bits]
    half = keep + xor_permute(send, 1, total)
    done = [steps[0]()]
    half = scatter_sum(half, me, bits, total)
    half, done[0] = lax.optimization_barrier((half, done[0]))
    done.append(steps[1](*done))
    for i in range(0, len(rest), 2):
        half = direct_sum(half, rest[i : i + 2], total)
    half, done[1] = lax.optimization_barrier((half, done[1]))
    done += [step(*done) for step in steps[2:]]
    half = gather(half, me, bits, total)
    if steps[2:]:
        half, done[2] = lax.optimization_barrier((half, done[2]))
    return half, xor_permute(half, 1, total), done


def per_device(n_ty, n_tx, table, object_field, probe, intensities, positions):
    win, modes = probe.shape[-1], probe.shape[1]
    margin, tile, scans = win // 2, object_field.shape[-1], positions.shape[2]
    spots = positions.reshape(scans, 2)
    measured = intensities.reshape(scans, win, win)
    match_y, match_x = pairings(n_ty), pairings(n_tx)
    n_y, n_x = len(match_y), len(match_x)
    odd_y = lax.axis_index("ty") % 2

    def swap(x, pairs_y, pairs_x):
        return lax.ppermute(x, AXES, flat_pairs(pairs_y, pairs_x, n_ty, n_tx))

    def rows_for(x, i, count, low, high):
        start = jnp.where(odd_y == i, high, low)
        return lax.dynamic_slice_in_dim(x, start, count, 1)

    tx_in = [swap(object_field, None, px) for px in match_x]
    rims = [rows_for(object_field, i, margin, 0, tile - margin) for i in range(n_y)]
    ty_in = [swap(rims[i], py, None) for i, py in enumerate(match_y)]
    corners = []
    for i, py in enumerate(match_y):
        corners += [swap(ty_in[i], None, px) for px in match_x[:1]]
        corners += [swap(rims[i], py, px) for px in match_x[1:]]

    shape_of = lambda x: jax.ShapeDtypeStruct(x.shape, x.dtype)
    ready = (probe, measured, jnp.asarray(table))
    ready = call(prepare_kernel, [shape_of(x) for x in ready], ready)
    (tx_in, ty_in, corners), (probe, root, table) = lax.optimization_barrier(
        ((tx_in, ty_in, corners), tuple(ready))
    )

    at_y, at_x = lax.axis_index("ty"), lax.axis_index("tx")
    half_shape = (modes, win + WEIGHT_ROWS, win)
    grid_shape = (2, 2 * tile + SUBLANES, 2 * tile)
    sent = [half_shape] * 2 + [object_field.shape] * 2 + [(2, 2, margin, tile)] * n_y
    scratch = [grid_shape, (2 * modes, win, win)]

    def exchanges(overlaps, rims):
        def folded(received):
            halves = [x.reshape(2, 2, margin, tile) for x in overlaps]
            place = lax.broadcasted_iota(jnp.int32, (1, 2, 1, 1), 1)
            for i, y in enumerate(received):
                here = place == jnp.where(odd_y == i, 1, 0)
                for k in (0, 1):
                    extra = if_paired(y[k][:, None], at_y, n_ty, i)
                    halves[k] = halves[k] + jnp.where(here, extra, 0.0)
            return [x.reshape(object_field.shape) for x in halves]

        def fold():
            return [swap(rim, py, None) for rim, py in zip(rims, match_y)]

        def across(received):
            mine = folded(received)
            return mine, [swap(x, None, px) for x, px in zip(mine, match_x)]

        def halo(received, columns):
            mine, theirs = columns
            total = list(mine)
            for i, x in enumerate(theirs):
                total[i] = total[i] + if_paired(x, at_x, n_tx, i)
            bands = [
                jnp.stack([rows_for(x, i, margin, 0, tile - margin) for x in total])
                for i in range(n_y)
            ]
            return [swap(band, py, None) for band, py in zip(bands, match_y)]

        return fold, across, halo

    ext, keep, send, first, second, *rims = call(
        functools.partial(first_kernel, n_ty, n_tx, n_y, n_x, margin),
        [grid_shape] + sent,
        [spots, object_field, probe, root, table, *ty_in, *tx_in, *corners],
        scratch,
    )
    steps = exchanges([first, second], rims)
    own, other, (_, (overlaps, tx_in), halo) = summed_halves(keep, send, n_ty, n_tx, steps)
    tile_mid, probe_mid, keep, send, first, second, *rims = call(
        functools.partial(second_kernel, n_ty, n_tx, n_y, n_x, margin),
        [object_field.shape, probe.shape] + sent,
        [spots, ext, *overlaps, probe, root, table, own, other, *tx_in, *halo],
        [grid_shape] + scratch,
    )
    steps = exchanges([first, second], rims)
    own, other, (_, (overlaps, tx_in)) = summed_halves(keep, send, n_ty, n_tx, steps[:2])
    return call(
        functools.partial(last_kernel, n_tx, n_x, margin),
        [object_field.shape, probe.shape],
        [tile_mid, *overlaps, probe_mid, own, other, *tx_in],
    )


def solution(mesh):
    n_ty, n_tx = mesh.shape["ty"], mesh.shape["tx"]
    placed = (P(None, "ty", "tx"), P(), P("ty", "tx", None, None, None), P("ty", "tx", None, None))

    def run(object_field, probe, intensities, positions):
        table = dft_table(probe.shape[-1])
        return jax.shard_map(
            functools.partial(per_device, n_ty, n_tx, table),
            mesh=mesh,
            in_specs=placed,
            out_specs=(P(None, "ty", "tx"), P()),
            check_vma=False,
        )(object_field, probe, intensities, positions)

    return run
```

```python
import functools

import jax
import jax.numpy as jnp
import numpy as np
from jax import lax
from jax.experimental import pallas as pl
from jax.experimental.pallas import tpu as pltpu
from jax.sharding import PartitionSpec as P

ROUNDS = 2
OBJECT_STEP = 0.1
PROBE_RELAX = 0.5
AXES = ("ty", "tx")
SUBLANES = 8
WEIGHT_ROWS = SUBLANES
F32 = jnp.float32
BF16 = jnp.bfloat16


def dft_table(win):
    line = np.arange(win, dtype=np.int64)
    angle = (line[:, None] * line[None, :] % win) * (2.0 * np.pi / win)
    full = (np.stack([np.cos(angle), np.sin(angle)]) / np.sqrt(win)).astype(np.float32)
    high = full.astype(jnp.bfloat16)
    low = (full - high.astype(np.float32)).astype(jnp.bfloat16)
    return np.concatenate([high, low])


def pairings(size):
    found = []
    for first in (0, 1):
        pairs = {}
        for low in range(first, size - 1, 2):
            pairs[low], pairs[low + 1] = low + 1, low
        if pairs:
            found.append(pairs)
    return found


def flat_pairs(pairs_y, pairs_x, n_ty, n_tx):
    out, alone = [], []
    for x in range(n_tx):
        for y in range(n_ty):
            to_y = y if pairs_y is None else pairs_y.get(y)
            to_x = x if pairs_x is None else pairs_x.get(x)
            if to_y is None or to_x is None:
                alone.append(y * n_tx + x)
            else:
                out.append((y * n_tx + x, to_y * n_tx + to_x))
    for a, b in zip(alone[::2], alone[1::2]):
        out += [(a, b), (b, a)]
    if len(alone) % 2:
        out.append((alone[-1], alone[-1]))
    return out


def if_paired(x, at, size, i):
    last = i + 2 * ((size - i) // 2)
    if i > 0:
        x = jnp.where(at >= i, x, 0.0)
    return jnp.where(at < last, x, 0.0) if last < size else x


def xor_permute(x, mask, total):
    return lax.ppermute(x, AXES, [(i, i ^ mask) for i in range(total)])


def split(x):
    high = x.astype(BF16)
    return high, (x - high.astype(F32)).astype(BF16)


def product(a, b):
    (a_high, a_low), (b_high, b_low) = a, b
    return jnp.dot(
        jnp.concatenate([a_high, a_low, a_high], axis=1),
        jnp.concatenate([b_high, b_high, b_low], axis=0),
        preferred_element_type=F32,
    )


def block(c, upper, lower):
    return jnp.concatenate(
        [jnp.concatenate([c, upper], axis=1), jnp.concatenate([lower, c], axis=1)], axis=0
    )


def lane_pick(width, margin, flag):
    lane = lax.broadcasted_iota(jnp.int32, (8, width), 1)
    below = jnp.where(lane < margin, 0, 1)
    return below == flag


def rowwise(mask, rows):
    return jnp.broadcast_to(mask[:1], (rows, mask.shape[1]))


def by_parity(odd, even_value, odd_value):
    return jnp.where(odd == 1, odd_value, even_value)


def compute(
    ext_ref, probe_ref, root_ref, pos_ref, table_ref, grid_ref, grad_ref, *, margin
):
    scans, win = root_ref.shape[0], root_ref.shape[1]
    modes = probe_ref.shape[1]
    width, tall = 2 * win, win + SUBLANES
    w_fwd = [block(table_ref[i], -table_ref[i + 1], table_ref[i + 1]) for i in (0, 2)]
    l_fwd = [block(table_ref[i], table_ref[i + 1], -table_ref[i + 1]) for i in (0, 2)]
    grid_ref[...] = jnp.zeros_like(grid_ref)
    windows, state, weights = {}, {}, []

    def corner(s):
        r, c = pos_ref[s, 0], pos_ref[s, 1]
        q = r % SUBLANES
        return pl.multiple_of(r - q, SUBLANES), q, c

    def enter(s):
        base, q, c = corner(s)
        turn = jnp.where(c <= margin, margin - c, margin + width - c)
        lift = jnp.where(q == 0, 0, tall - q)

        def window(part):
            band = pltpu.roll(ext_ref[part, pl.ds(base, tall), :], turn, 1)[:, :win]
            return pltpu.roll(band, lift, 0)[:win]

        o_re, o_im = windows[s] = window(0), window(1)
        power = o_re * o_re + o_im * o_im
        weights.append(jnp.sum(power.reshape(win // WEIGHT_ROWS, WEIGHT_ROWS, win), axis=0))
        rows = []
        for k in range(modes):
            p_re, p_im = probe_ref[0, k], probe_ref[1, k]
            rows.append(
                jnp.concatenate([p_re * o_re - p_im * o_im, p_re * o_im + p_im * o_re], axis=1)
            )
        state[s] = product(split(jnp.concatenate(rows, axis=0)), w_fwd)

    def forward(s):
        y = state[s]
        y = jnp.concatenate(
            [
                jnp.concatenate([y[k * win : (k + 1) * win, :win] for k in range(modes)], axis=1),
                jnp.concatenate([y[k * win : (k + 1) * win, win:] for k in range(modes)], axis=1),
            ],
            axis=0,
        )
        state[s] = product(l_fwd, split(y))

    def scale(s):
        far = state[s]
        square = far * far
        square = square[:win] + square[win:]
        total = square[:, :win]
        for k in range(1, modes):
            total = total + square[:, k * win : (k + 1) * win]
        ratio = root_ref[s] * lax.rsqrt(jnp.maximum(total, 1.0)) - 1.0
        ratio = jnp.concatenate([ratio] * modes, axis=1)
        far = far * jnp.concatenate([ratio, ratio], axis=0)
        state[s] = product(w_fwd, split(far))

    def backward(s):
        u = state[s]
        u = jnp.concatenate(
            [
                jnp.concatenate(
                    [u[:win, k * win : (k + 1) * win], u[win:, k * win : (k + 1) * win]], axis=1
                )
                for k in range(modes)
            ],
            axis=0,
        )
        state[s] = product(split(u), l_fwd)

    def leave(s):
        chi = state[s]
        o_re, o_im = windows[s]
        g_re = g_im = None
        for k in range(modes):
            p_re, p_im = probe_ref[0, k], probe_ref[1, k]
            c_re, c_im = chi[k * win : (k + 1) * win, :win], chi[k * win : (k + 1) * win, win:]
            a, b = p_re * c_re + p_im * c_im, p_re * c_im - p_im * c_re
            g_re, g_im = (a, b) if k == 0 else (g_re + a, g_im + b)
            a, b = o_re * c_re + o_im * c_im, o_re * c_im - o_im * c_re
            if s == 0:
                grad_ref[k], grad_ref[modes + k] = a, b
            else:
                grad_ref[k] += a
                grad_ref[modes + k] += b
        base, q, c = corner(s)
        back = jnp.where(c >= margin, c - margin, c + width - margin)
        for part, g in ((0, g_re), (1, g_im)):
            g = pltpu.roll(jnp.concatenate([g, jnp.zeros((SUBLANES, win), F32)], axis=0), q, 0)
            g = jnp.concatenate([g, jnp.zeros_like(g)], axis=1)
            grid_ref[part, pl.ds(base, tall), :] += pltpu.roll(g, back, 1)

    stages = (enter, forward, scale, backward, leave)
    for stage in stages:
        for s in range(scans):
            stage(s)
    return functools.reduce(jnp.add, weights)


def emit(grad_ref, weight, grid_ref, keep_ref, send_ref, first_ref, second_ref, rim_refs, margin):
    count, win = keep_ref.shape[0], grad_ref.shape[1]
    odd_y, odd_x = lax.axis_index("ty") % 2, lax.axis_index("tx") % 2
    for j in range(count):
        keep_ref[j, :win, :] = grad_ref[odd_x * count + j]
        send_ref[j, :win, :] = grad_ref[(1 - odd_x) * count + j]
        keep_ref[j, win:, :] = weight
        send_ref[j, win:, :] = weight
    tile = first_ref.shape[-1]
    mask = rowwise(lane_pick(tile, margin, odd_x), tile)
    for part in (0, 1):
        rows = grid_ref[part, margin : margin + tile, :]
        first_ref[part], second_ref[part] = chosen(mask, rows[:, tile:], rows[:, :tile])
        for i, ref in enumerate(rim_refs):
            start = pl.multiple_of(jnp.where(odd_y == i, 2 * tile - margin, 0), margin)
            rows = grid_ref[part, pl.ds(start, margin), :]
            ref[0, part], ref[1, part] = chosen(mask[:margin], rows[:, tile:], rows[:, :tile])


def chosen(mask, a, b):
    return jnp.where(mask, a, b), jnp.where(mask, b, a)


def prepare_kernel(probe_ref, meas_ref, table_ref, probe_out, root_ref, table_out):
    probe_out[...] = probe_ref[...]
    root_ref[...] = jnp.sqrt(meas_ref[...])
    table_out[...] = table_ref[...]


def first_kernel(n_ty, n_tx, n_y, n_x, margin, pos_ref, obj_ref, probe_ref, root_ref, table_ref, *rest):
    take = iter(rest)
    ty_refs = [next(take) for _ in range(n_y)]
    tx_refs = [next(take) for _ in range(n_x)]
    corner_refs = [[next(take) for _ in range(n_x)] for _ in range(n_y)]
    ext_ref, keep_ref, send_ref, first_ref, second_ref, *rim_refs = take
    *rim_refs, grid_ref, grad_ref = rim_refs
    tile = obj_ref.shape[-1]
    at_y, at_x = lax.axis_index("ty"), lax.axis_index("tx")
    odd_y, odd_x = at_y % 2, at_x % 2
    pick = lane_pick(tile, margin, odd_x)

    def side(refs, part, rows):
        both = [if_paired(ref[part], at_x, n_tx, i) for i, ref in enumerate(refs)]
        both += [jnp.zeros((rows, tile), F32)] * (2 - n_x)
        return jnp.where(rowwise(pick, rows), both[0], both[1])

    for part in (0, 1):
        ext_ref[part, margin : margin + tile, :tile] = obj_ref[part]
        ext_ref[part, margin : margin + tile, tile:] = side(tx_refs, part, tile)
        bands = [
            if_paired(
                jnp.concatenate([ty_refs[i][part], side(corner_refs[i], part, margin)], axis=1),
                at_y, n_ty, i,
            )
            for i in range(n_y)
        ]
        bands += [jnp.zeros((margin, 2 * tile), F32)] * (2 - n_y)
        ext_ref[part, :margin, :] = by_parity(odd_y, bands[1], bands[0])
        ext_ref[part, margin + tile : 2 * tile, :] = by_parity(odd_y, bands[0], bands[1])
    weight = compute(
        ext_ref, probe_ref, root_ref, pos_ref, table_ref, grid_ref, grad_ref, margin=margin
    )
    emit(
        grad_ref, weight, grid_ref, keep_ref, send_ref, first_ref, second_ref, rim_refs, margin
    )


def combined_probe(probe_ref, own_ref, other_ref, new_ref, half):
    count, win, modes = own_ref.shape[0], probe_ref.shape[-1], probe_ref.shape[1]
    weight = jnp.sum(own_ref[0, win:, :])
    scale = PROBE_RELAX * win * win / jnp.full((8, win), weight, F32)
    scale = jnp.broadcast_to(scale[:1], (win, win))
    for j in range(count):
        for ref, index in ((own_ref, half * count + j), (other_ref, (1 - half) * count + j)):
            part, k = index // modes, index % modes
            new_ref[part, k] = probe_ref[part, k] + scale * ref[j, :win, :]


def second_kernel(
    n_ty, n_tx, n_y, n_x, margin, pos_ref, old_ref, first_ref, second_ref, probe_ref, root_ref,
    table_ref, own_ref, other_ref, *rest
):
    take = iter(rest)
    tx_refs = [next(take) for _ in range(n_x)]
    halo_refs = [next(take) for _ in range(n_y)]
    tile_ref, new_ref, keep_ref, send_ref, next_first_ref, next_second_ref, *rim_refs = take
    *rim_refs, ext_ref, grid_ref, grad_ref = rim_refs
    tile = probe_ref.shape[-1]
    at_y, at_x = lax.axis_index("ty"), lax.axis_index("tx")
    odd_y, odd_x = at_y % 2, at_x % 2
    combined_probe(probe_ref, own_ref, other_ref, new_ref, odd_x)
    row = lax.broadcasted_iota(jnp.int32, (2 * tile, 2 * tile), 0)
    lane = lax.broadcasted_iota(jnp.int32, (2 * tile, 2 * tile), 1)
    inside = (row >= jnp.where(at_y == 0, margin, 0)) & (
        row < jnp.where(at_y == n_ty - 1, margin + tile, 2 * tile)
    )
    inside &= (lane < jnp.where(at_x == n_tx - 1, tile, tile + margin)) | (
        lane >= jnp.where(at_x == 0, 2 * tile, tile + margin)
    )
    mask = rowwise(lane_pick(tile, margin, odd_x), tile)
    for i in range(2):
        start = pl.multiple_of(jnp.where(odd_y == i, margin + tile, 0), margin)
        for part in (0, 1):
            if i < n_y:
                ref = halo_refs[i]
                own, margins = chosen(mask[:margin], ref[1, part], ref[0, part])
                rows = jnp.concatenate([own, margins], axis=1)
            else:
                rows = jnp.zeros((margin, 2 * tile), F32)
            ext_ref[part, pl.ds(start, margin), :] = rows
    for part in (0, 1):
        both = [first_ref[part], second_ref[part]]
        for i, ref in enumerate(tx_refs):
            both[i] = both[i] + if_paired(ref[part], at_x, n_tx, i)
        own, margins = chosen(mask, both[1], both[0])
        ext_ref[part, margin : margin + tile, :] = jnp.concatenate([own, margins], axis=1)
        step = jnp.where(inside, OBJECT_STEP * ext_ref[part, : 2 * tile, :], 0.0)
        ext_ref[part, : 2 * tile, :] = old_ref[part, : 2 * tile, :] + step
        tile_ref[part] = ext_ref[part, margin : margin + tile, :tile]
    weight = compute(
        ext_ref, new_ref, root_ref, pos_ref, table_ref, grid_ref, grad_ref, margin=margin
    )
    emit(
        grad_ref, weight, grid_ref, keep_ref, send_ref, next_first_ref, next_second_ref, rim_refs,
        margin,
    )


def last_kernel(
    n_tx, n_x, margin, tile_ref, first_ref, second_ref, probe_ref, own_ref, other_ref, *rest
):
    *tx_refs, obj_ref, new_ref = rest
    tile = tile_ref.shape[-1]
    at_x = lax.axis_index("tx")
    combined_probe(probe_ref, own_ref, other_ref, new_ref, at_x % 2)
    mask = rowwise(lane_pick(tile, margin, at_x % 2), tile)
    for part in (0, 1):
        both = [first_ref[part], second_ref[part]]
        for i, ref in enumerate(tx_refs):
            both[i] = both[i] + if_paired(ref[part], at_x, n_tx, i)
        obj_ref[part] = tile_ref[part] + OBJECT_STEP * chosen(mask, both[1], both[0])[0]


def call(kernel, outs, ins, scratch=()):
    smem = pl.BlockSpec(memory_space=pltpu.SMEM)
    vmem = pl.BlockSpec(memory_space=pltpu.VMEM)
    shapes = [s if hasattr(s, "dtype") else jax.ShapeDtypeStruct(s, F32) for s in outs]
    return pl.pallas_call(
        kernel,
        out_shape=shapes,
        in_specs=[smem if x.dtype == jnp.int32 else vmem for x in ins],
        out_specs=[vmem] * len(outs),
        scratch_shapes=[pltpu.VMEM(s, F32) for s in scratch],
        compiler_params=pltpu.CompilerParams(vmem_limit_bytes=16 * 1024 * 1024),
    )(*ins)


def bit_of(me, bit):
    return (me >> bit) & 1


def masks_of(bits):
    return [sum(((m >> i) & 1) << b for i, b in enumerate(bits)) for m in range(1, 1 << len(bits))]


def local_index(me, bits):
    return sum(bit_of(me, b) << i for i, b in enumerate(bits))


def tree(values):
    while len(values) > 1:
        values = [a + b for a, b in zip(values[::2], values[1::2])] + values[len(values) & ~1 :]
    return values[0]


def scatter_sum(x, me, bits, total, beside):
    here = local_index(me, bits)
    n = 1 << len(bits)
    x = x.reshape((n, x.shape[0] // n) + x.shape[1:])
    parts = [lax.dynamic_index_in_dim(x, here, 0, False)]
    for m, mask in enumerate(masks_of(bits), 1):
        parts.append(xor_permute(lax.dynamic_index_in_dim(x, here ^ m, 0, False), mask, total))
    parts[0], beside = lax.optimization_barrier((parts[0], beside))
    return tree(parts), beside


def direct_sum(x, bits, total, beside):
    parts = [xor_permute(x, mask, total) for mask in masks_of(bits)]
    x, beside = lax.optimization_barrier((x, beside))
    return tree([x] + parts), beside


def gather(x, me, bits, total):
    here = local_index(me, bits)
    parts = jnp.stack([x] + [xor_permute(x, mask, total) for mask in masks_of(bits)])
    return jnp.concatenate(
        [lax.dynamic_index_in_dim(parts, here ^ j, 0, False) for j in range(1 << len(bits))]
    )


def summed_halves(keep, send, n_ty, n_tx, steps):
    total = n_ty * n_tx
    me = lax.axis_index("ty") * n_tx + lax.axis_index("tx")
    levels = total.bit_length() - 1
    tx_bits = n_tx.bit_length() - 1
    bits = [b for b in (tx_bits, 1) if b < levels]
    rest = [b for b in range(1, levels) if b not in bits]
    half = keep + xor_permute(send, 1, total)
    done = [steps[0]()]
    half, done[0] = scatter_sum(half, me, bits, total, done[0])
    done.append(steps[1](*done))
    for i in range(0, len(rest), 2):
        half, _ = direct_sum(half, rest[i : i + 2], total, ())
    half, done[1] = lax.optimization_barrier((half, done[1]))
    done += [step(*done) for step in steps[2:]]
    half = gather(half, me, bits, total)
    if steps[2:]:
        half, done[2] = lax.optimization_barrier((half, done[2]))
    return half, xor_permute(half, 1, total), done


def per_device(n_ty, n_tx, table, object_field, probe, intensities, positions):
    win, modes = probe.shape[-1], probe.shape[1]
    margin, tile, scans = win // 2, object_field.shape[-1], positions.shape[2]
    spots = positions.reshape(scans, 2)
    measured = intensities.reshape(scans, win, win)
    match_y, match_x = pairings(n_ty), pairings(n_tx)
    n_y, n_x = len(match_y), len(match_x)
    odd_y = lax.axis_index("ty") % 2

    def swap(x, pairs_y, pairs_x):
        return lax.ppermute(x, AXES, flat_pairs(pairs_y, pairs_x, n_ty, n_tx))

    def rows_for(x, i, count, low, high):
        start = jnp.where(odd_y == i, high, low)
        return lax.dynamic_slice_in_dim(x, start, count, 1)

    tx_in = [swap(object_field, None, px) for px in match_x]
    rims = [rows_for(object_field, i, margin, 0, tile - margin) for i in range(n_y)]
    ty_in = [swap(rims[i], py, None) for i, py in enumerate(match_y)]
    corners = []
    for i, py in enumerate(match_y):
        corners += [swap(ty_in[i], None, px) for px in match_x[:1]]
        corners += [swap(rims[i], py, px) for px in match_x[1:]]

    shape_of = lambda x: jax.ShapeDtypeStruct(x.shape, x.dtype)
    ready = (probe, measured, jnp.asarray(table))
    ready = call(prepare_kernel, [shape_of(x) for x in ready], ready)
    (tx_in, ty_in, corners), (probe, root, table) = lax.optimization_barrier(
        ((tx_in, ty_in, corners), tuple(ready))
    )

    at_y, at_x = lax.axis_index("ty"), lax.axis_index("tx")
    half_shape = (modes, win + WEIGHT_ROWS, win)
    grid_shape = (2, 2 * tile + SUBLANES, 2 * tile)
    sent = [half_shape] * 2 + [object_field.shape] * 2 + [(2, 2, margin, tile)] * n_y
    scratch = [grid_shape, (2 * modes, win, win)]

    def exchanges(overlaps, rims):
        def folded(received):
            halves = [x.reshape(2, 2, margin, tile) for x in overlaps]
            place = lax.broadcasted_iota(jnp.int32, (1, 2, 1, 1), 1)
            for i, y in enumerate(received):
                here = place == jnp.where(odd_y == i, 1, 0)
                for k in (0, 1):
                    extra = if_paired(y[k][:, None], at_y, n_ty, i)
                    halves[k] = halves[k] + jnp.where(here, extra, 0.0)
            return [x.reshape(object_field.shape) for x in halves]

        def fold():
            return [swap(rim, py, None) for rim, py in zip(rims, match_y)]

        def across(received):
            mine = folded(received)
            return mine, [swap(x, None, px) for x, px in zip(mine, match_x)]

        def halo(received, columns):
            mine, theirs = columns
            total = list(mine)
            for i, x in enumerate(theirs):
                total[i] = total[i] + if_paired(x, at_x, n_tx, i)
            bands = [
                jnp.stack([rows_for(x, i, margin, 0, tile - margin) for x in total])
                for i in range(n_y)
            ]
            return [swap(band, py, None) for band, py in zip(bands, match_y)]

        return fold, across, halo

    ext, keep, send, first, second, *rims = call(
        functools.partial(first_kernel, n_ty, n_tx, n_y, n_x, margin),
        [grid_shape] + sent,
        [spots, object_field, probe, root, table, *ty_in, *tx_in, *corners],
        scratch,
    )
    steps = exchanges([first, second], rims)
    own, other, (_, (overlaps, tx_in), halo) = summed_halves(keep, send, n_ty, n_tx, steps)
    tile_mid, probe_mid, keep, send, first, second, *rims = call(
        functools.partial(second_kernel, n_ty, n_tx, n_y, n_x, margin),
        [object_field.shape, probe.shape] + sent,
        [spots, ext, *overlaps, probe, root, table, own, other, *tx_in, *halo],
        [grid_shape] + scratch,
    )
    steps = exchanges([first, second], rims)
    own, other, (_, (overlaps, tx_in)) = summed_halves(keep, send, n_ty, n_tx, steps[:2])
    return call(
        functools.partial(last_kernel, n_tx, n_x, margin),
        [object_field.shape, probe.shape],
        [tile_mid, *overlaps, probe_mid, own, other, *tx_in],
    )


def solution(mesh):
    n_ty, n_tx = mesh.shape["ty"], mesh.shape["tx"]
    placed = (P(None, "ty", "tx"), P(), P("ty", "tx", None, None, None), P("ty", "tx", None, None))

    def run(object_field, probe, intensities, positions):
        table = dft_table(probe.shape[-1])
        return jax.shard_map(
            functools.partial(per_device, n_ty, n_tx, table),
            mesh=mesh,
            in_specs=placed,
            out_specs=(P(None, "ty", "tx"), P()),
            check_vma=False,
        )(object_field, probe, intensities, positions)

    return run
```

```python
import functools

import jax
import jax.numpy as jnp
import numpy as np
from jax import lax
from jax.experimental import pallas as pl
from jax.experimental.pallas import tpu as pltpu
from jax.sharding import PartitionSpec as P

ROUNDS = 2
OBJECT_STEP = 0.1
PROBE_RELAX = 0.5
AXES = ("ty", "tx")
SUBLANES = 8
WEIGHT_ROWS = SUBLANES
F32 = jnp.float32
BF16 = jnp.bfloat16


def dft_table(win):
    line = np.arange(win, dtype=np.int64)
    angle = (line[:, None] * line[None, :] % win) * (2.0 * np.pi / win)
    full = (np.stack([np.cos(angle), np.sin(angle)]) / np.sqrt(win)).astype(np.float32)
    high = full.astype(jnp.bfloat16)
    low = (full - high.astype(np.float32)).astype(jnp.bfloat16)
    return np.concatenate([high, low])


def pairings(size):
    found = []
    for first in (0, 1):
        pairs = {}
        for low in range(first, size - 1, 2):
            pairs[low], pairs[low + 1] = low + 1, low
        if pairs:
            found.append(pairs)
    return found


def flat_pairs(pairs_y, pairs_x, n_ty, n_tx):
    out, alone = [], []
    for x in range(n_tx):
        for y in range(n_ty):
            to_y = y if pairs_y is None else pairs_y.get(y)
            to_x = x if pairs_x is None else pairs_x.get(x)
            if to_y is None or to_x is None:
                alone.append(y * n_tx + x)
            else:
                out.append((y * n_tx + x, to_y * n_tx + to_x))
    for a, b in zip(alone[::2], alone[1::2]):
        out += [(a, b), (b, a)]
    if len(alone) % 2:
        out.append((alone[-1], alone[-1]))
    return out


def if_paired(x, at, size, i):
    last = i + 2 * ((size - i) // 2)
    if i > 0:
        x = jnp.where(at >= i, x, 0.0)
    return jnp.where(at < last, x, 0.0) if last < size else x


def xor_permute(x, mask, total):
    return lax.ppermute(x, AXES, [(i, i ^ mask) for i in range(total)])


def split(x):
    high = x.astype(BF16)
    return high, (x - high.astype(F32)).astype(BF16)


def product(a, b):
    (a_high, a_low), (b_high, b_low) = a, b
    return jnp.dot(
        jnp.concatenate([a_high, a_low, a_high], axis=1),
        jnp.concatenate([b_high, b_high, b_low], axis=0),
        preferred_element_type=F32,
    )


def block(c, upper, lower):
    return jnp.concatenate(
        [jnp.concatenate([c, upper], axis=1), jnp.concatenate([lower, c], axis=1)], axis=0
    )


def lane_pick(width, margin, flag):
    lane = lax.broadcasted_iota(jnp.int32, (8, width), 1)
    below = jnp.where(lane < margin, 0, 1)
    return below == flag


def rowwise(mask, rows):
    return jnp.broadcast_to(mask[:1], (rows, mask.shape[1]))


def by_parity(odd, even_value, odd_value):
    return jnp.where(odd == 1, odd_value, even_value)


def compute(
    ext_ref, probe_ref, root_ref, pos_ref, table_ref, grid_ref, grad_ref, *, margin
):
    scans, win = root_ref.shape[0], root_ref.shape[1]
    modes = probe_ref.shape[1]
    width, tall = 2 * win, win + SUBLANES
    w_fwd = [block(table_ref[i], -table_ref[i + 1], table_ref[i + 1]) for i in (0, 2)]
    l_fwd = [block(table_ref[i], table_ref[i + 1], -table_ref[i + 1]) for i in (0, 2)]
    grid_ref[...] = jnp.zeros_like(grid_ref)
    windows, state, weights = {}, {}, []

    def corner(s):
        r, c = pos_ref[s, 0], pos_ref[s, 1]
        q = r % SUBLANES
        return pl.multiple_of(r - q, SUBLANES), q, c

    def enter(s):
        base, q, c = corner(s)
        turn = jnp.where(c <= margin, margin - c, margin + width - c)
        lift = jnp.where(q == 0, 0, tall - q)

        def window(part):
            band = pltpu.roll(ext_ref[part, pl.ds(base, tall), :], turn, 1)[:, :win]
            return pltpu.roll(band, lift, 0)[:win]

        o_re, o_im = windows[s] = window(0), window(1)
        power = o_re * o_re + o_im * o_im
        weights.append(jnp.sum(power.reshape(win // WEIGHT_ROWS, WEIGHT_ROWS, win), axis=0))
        rows = []
        for k in range(modes):
            p_re, p_im = probe_ref[0, k], probe_ref[1, k]
            rows.append(
                jnp.concatenate([p_re * o_re - p_im * o_im, p_re * o_im + p_im * o_re], axis=1)
            )
        state[s] = product(split(jnp.concatenate(rows, axis=0)), w_fwd)

    def forward(s):
        y = state[s]
        y = jnp.concatenate(
            [
                jnp.concatenate([y[k * win : (k + 1) * win, :win] for k in range(modes)], axis=1),
                jnp.concatenate([y[k * win : (k + 1) * win, win:] for k in range(modes)], axis=1),
            ],
            axis=0,
        )
        state[s] = product(l_fwd, split(y))

    def scale(s):
        far = state[s]
        square = far * far
        square = square[:win] + square[win:]
        total = square[:, :win]
        for k in range(1, modes):
            total = total + square[:, k * win : (k + 1) * win]
        ratio = root_ref[s] * lax.rsqrt(jnp.maximum(total, 1.0)) - 1.0
        ratio = jnp.concatenate([ratio] * modes, axis=1)
        far = far * jnp.concatenate([ratio, ratio], axis=0)
        state[s] = product(w_fwd, split(far))

    def backward(s):
        u = state[s]
        u = jnp.concatenate(
            [
                jnp.concatenate(
                    [u[:win, k * win : (k + 1) * win], u[win:, k * win : (k + 1) * win]], axis=1
                )
                for k in range(modes)
            ],
            axis=0,
        )
        state[s] = product(split(u), l_fwd)

    def leave(s):
        chi = state[s]
        o_re, o_im = windows[s]
        g_re = g_im = None
        for k in range(modes):
            p_re, p_im = probe_ref[0, k], probe_ref[1, k]
            c_re, c_im = chi[k * win : (k + 1) * win, :win], chi[k * win : (k + 1) * win, win:]
            a, b = p_re * c_re + p_im * c_im, p_re * c_im - p_im * c_re
            g_re, g_im = (a, b) if k == 0 else (g_re + a, g_im + b)
            a, b = o_re * c_re + o_im * c_im, o_re * c_im - o_im * c_re
            if s == 0:
                grad_ref[k], grad_ref[modes + k] = a, b
            else:
                grad_ref[k] += a
                grad_ref[modes + k] += b
        base, q, c = corner(s)
        back = jnp.where(c >= margin, c - margin, c + width - margin)
        for part, g in ((0, g_re), (1, g_im)):
            g = pltpu.roll(jnp.concatenate([g, jnp.zeros((SUBLANES, win), F32)], axis=0), q, 0)
            g = jnp.concatenate([g, jnp.zeros_like(g)], axis=1)
            grid_ref[part, pl.ds(base, tall), :] += pltpu.roll(g, back, 1)

    stages = (enter, forward, scale, backward, leave)
    for stage in stages:
        for s in range(scans):
            stage(s)
    return functools.reduce(jnp.add, weights)


def emit(grad_ref, weight, grid_ref, keep_ref, send_ref, first_ref, second_ref, rim_refs, margin):
    count, win = keep_ref.shape[0], grad_ref.shape[1]
    odd_y, odd_x = lax.axis_index("ty") % 2, lax.axis_index("tx") % 2
    for j in range(count):
        keep_ref[j, :win, :] = grad_ref[odd_x * count + j]
        send_ref[j, :win, :] = grad_ref[(1 - odd_x) * count + j]
        keep_ref[j, win:, :] = weight
        send_ref[j, win:, :] = weight
    tile = first_ref.shape[-1]
    mask = rowwise(lane_pick(tile, margin, odd_x), tile)
    for part in (0, 1):
        rows = grid_ref[part, margin : margin + tile, :]
        first_ref[part], second_ref[part] = chosen(mask, rows[:, tile:], rows[:, :tile])
        for i, ref in enumerate(rim_refs):
            start = pl.multiple_of(jnp.where(odd_y == i, 2 * tile - margin, 0), margin)
            rows = grid_ref[part, pl.ds(start, margin), :]
            ref[0, part], ref[1, part] = chosen(mask[:margin], rows[:, tile:], rows[:, :tile])


def chosen(mask, a, b):
    return jnp.where(mask, a, b), jnp.where(mask, b, a)


def prepare_kernel(probe_ref, meas_ref, table_ref, probe_out, root_ref, table_out):
    probe_out[...] = probe_ref[...]
    root_ref[...] = jnp.sqrt(meas_ref[...])
    table_out[...] = table_ref[...]


def first_kernel(n_ty, n_tx, n_y, n_x, margin, pos_ref, obj_ref, probe_ref, root_ref, table_ref, *rest):
    take = iter(rest)
    ty_refs = [next(take) for _ in range(n_y)]
    tx_refs = [next(take) for _ in range(n_x)]
    corner_refs = [[next(take) for _ in range(n_x)] for _ in range(n_y)]
    ext_ref, keep_ref, send_ref, first_ref, second_ref, *rim_refs = take
    *rim_refs, grid_ref, grad_ref = rim_refs
    tile = obj_ref.shape[-1]
    at_y, at_x = lax.axis_index("ty"), lax.axis_index("tx")
    odd_y, odd_x = at_y % 2, at_x % 2
    pick = lane_pick(tile, margin, odd_x)

    def side(refs, part, rows):
        both = [if_paired(ref[part], at_x, n_tx, i) for i, ref in enumerate(refs)]
        both += [jnp.zeros((rows, tile), F32)] * (2 - n_x)
        return jnp.where(rowwise(pick, rows), both[0], both[1])

    for part in (0, 1):
        ext_ref[part, margin : margin + tile, :tile] = obj_ref[part]
        ext_ref[part, margin : margin + tile, tile:] = side(tx_refs, part, tile)
        bands = [
            if_paired(
                jnp.concatenate([ty_refs[i][part], side(corner_refs[i], part, margin)], axis=1),
                at_y, n_ty, i,
            )
            for i in range(n_y)
        ]
        bands += [jnp.zeros((margin, 2 * tile), F32)] * (2 - n_y)
        ext_ref[part, :margin, :] = by_parity(odd_y, bands[1], bands[0])
        ext_ref[part, margin + tile : 2 * tile, :] = by_parity(odd_y, bands[0], bands[1])
    weight = compute(
        ext_ref, probe_ref, root_ref, pos_ref, table_ref, grid_ref, grad_ref, margin=margin
    )
    emit(
        grad_ref, weight, grid_ref, keep_ref, send_ref, first_ref, second_ref, rim_refs, margin
    )


def combined_probe(probe_ref, own_ref, other_ref, new_ref, half):
    count, win, modes = own_ref.shape[0], probe_ref.shape[-1], probe_ref.shape[1]
    weight = jnp.sum(own_ref[0, win:, :])
    scale = PROBE_RELAX * win * win / jnp.full((8, win), weight, F32)
    scale = jnp.broadcast_to(scale[:1], (win, win))
    for j in range(count):
        for ref, index in ((own_ref, half * count + j), (other_ref, (1 - half) * count + j)):
            part, k = index // modes, index % modes
            new_ref[part, k] = probe_ref[part, k] + scale * ref[j, :win, :]


def second_kernel(
    n_ty, n_tx, n_y, n_x, margin, pos_ref, old_ref, first_ref, second_ref, probe_ref, root_ref,
    table_ref, own_ref, other_ref, *rest
):
    take = iter(rest)
    tx_refs = [next(take) for _ in range(n_x)]
    halo_refs = [next(take) for _ in range(n_y)]
    tile_ref, new_ref, keep_ref, send_ref, next_first_ref, next_second_ref, *rim_refs = take
    *rim_refs, ext_ref, grid_ref, grad_ref = rim_refs
    tile = probe_ref.shape[-1]
    at_y, at_x = lax.axis_index("ty"), lax.axis_index("tx")
    odd_y, odd_x = at_y % 2, at_x % 2
    combined_probe(probe_ref, own_ref, other_ref, new_ref, odd_x)
    row = lax.broadcasted_iota(jnp.int32, (2 * tile, 2 * tile), 0)
    lane = lax.broadcasted_iota(jnp.int32, (2 * tile, 2 * tile), 1)
    inside = (row >= jnp.where(at_y == 0, margin, 0)) & (
        row < jnp.where(at_y == n_ty - 1, margin + tile, 2 * tile)
    )
    inside &= (lane < jnp.where(at_x == n_tx - 1, tile, tile + margin)) | (
        lane >= jnp.where(at_x == 0, 2 * tile, tile + margin)
    )
    mask = rowwise(lane_pick(tile, margin, odd_x), tile)
    for i in range(2):
        start = pl.multiple_of(jnp.where(odd_y == i, margin + tile, 0), margin)
        for part in (0, 1):
            if i < n_y:
                ref = halo_refs[i]
                own, margins = chosen(mask[:margin], ref[1, part], ref[0, part])
                rows = jnp.concatenate([own, margins], axis=1)
            else:
                rows = jnp.zeros((margin, 2 * tile), F32)
            ext_ref[part, pl.ds(start, margin), :] = rows
    for part in (0, 1):
        both = [first_ref[part], second_ref[part]]
        for i, ref in enumerate(tx_refs):
            both[i] = both[i] + if_paired(ref[part], at_x, n_tx, i)
        own, margins = chosen(mask, both[1], both[0])
        ext_ref[part, margin : margin + tile, :] = jnp.concatenate([own, margins], axis=1)
        step = jnp.where(inside, OBJECT_STEP * ext_ref[part, : 2 * tile, :], 0.0)
        ext_ref[part, : 2 * tile, :] = old_ref[part, : 2 * tile, :] + step
        tile_ref[part] = ext_ref[part, margin : margin + tile, :tile]
    weight = compute(
        ext_ref, new_ref, root_ref, pos_ref, table_ref, grid_ref, grad_ref, margin=margin
    )
    emit(
        grad_ref, weight, grid_ref, keep_ref, send_ref, next_first_ref, next_second_ref, rim_refs,
        margin,
    )


def last_kernel(
    n_tx, n_x, margin, tile_ref, first_ref, second_ref, probe_ref, own_ref, other_ref, *rest
):
    *tx_refs, obj_ref, new_ref = rest
    tile = tile_ref.shape[-1]
    at_x = lax.axis_index("tx")
    combined_probe(probe_ref, own_ref, other_ref, new_ref, at_x % 2)
    mask = rowwise(lane_pick(tile, margin, at_x % 2), tile)
    for part in (0, 1):
        both = [first_ref[part], second_ref[part]]
        for i, ref in enumerate(tx_refs):
            both[i] = both[i] + if_paired(ref[part], at_x, n_tx, i)
        obj_ref[part] = tile_ref[part] + OBJECT_STEP * chosen(mask, both[1], both[0])[0]


def call(kernel, outs, ins, scratch=()):
    smem = pl.BlockSpec(memory_space=pltpu.SMEM)
    vmem = pl.BlockSpec(memory_space=pltpu.VMEM)
    shapes = [s if hasattr(s, "dtype") else jax.ShapeDtypeStruct(s, F32) for s in outs]
    return pl.pallas_call(
        kernel,
        out_shape=shapes,
        in_specs=[smem if x.dtype == jnp.int32 else vmem for x in ins],
        out_specs=[vmem] * len(outs),
        scratch_shapes=[pltpu.VMEM(s, F32) for s in scratch],
        compiler_params=pltpu.CompilerParams(vmem_limit_bytes=16 * 1024 * 1024),
    )(*ins)


def bit_of(me, bit):
    return (me >> bit) & 1


def mask_of(bits, m):
    return sum(((m >> i) & 1) << b for i, b in enumerate(bits))


def swap_over(x, bits, m, total):
    masks = [mask_of(b, m) for b in bits]
    return lax.ppermute(x, AXES, [(i, i ^ masks[i & 1]) for i in range(total)])


def local_index(me, bits):
    even, odd = (sum(bit_of(me, b) << i for i, b in enumerate(side)) for side in bits)
    return even if bits[0] == bits[1] else jnp.where(me & 1 == 0, even, odd)


def tree(values):
    while len(values) > 1:
        values = [a + b for a, b in zip(values[::2], values[1::2])] + values[len(values) & ~1 :]
    return values[0]


def scatter_sum(x, me, bits, total, beside):
    here = local_index(me, bits)
    n = 1 << len(bits[0])
    x = x.reshape((n, x.shape[0] // n) + x.shape[1:])
    parts = [lax.dynamic_index_in_dim(x, here, 0, False)]
    for m in range(1, n):
        part = lax.dynamic_index_in_dim(x, here ^ m, 0, False)
        parts.append(swap_over(part, bits, m, total))
    parts[0], beside = lax.optimization_barrier((parts[0], beside))
    return tree(parts), beside


def direct_sum(x, bits, total):
    return tree([x] + [swap_over(x, bits, m, total) for m in range(1, 1 << len(bits[0]))])


def gather(x, me, bits, total, beside):
    here = local_index(me, bits)
    n = 1 << len(bits[0])
    parts = [swap_over(x, bits, m, total) for m in range(1, n)]
    x, beside = lax.optimization_barrier((x, beside))
    parts = jnp.stack([x] + parts)
    whole = [lax.dynamic_index_in_dim(parts, here ^ j, 0, False) for j in range(n)]
    return jnp.concatenate(whole), beside


def stages_of(n_ty, n_tx):
    levels, tx_bits = (n_ty * n_tx).bit_length() - 1, n_tx.bit_length() - 1
    near = tuple(b for b in dict.fromkeys((tx_bits, 1)) if b < levels)
    rest = [b for b in range(1, levels) if b not in near]
    far = tuple(rest[:2])
    if len(near) == len(far):
        return (near, far), [(far, near)] + [((b,), (b,)) for b in rest[2:]]
    return (near, near), [((b,), (b,)) for b in rest]


def summed_halves(keep, send, n_ty, n_tx, steps):
    total = n_ty * n_tx
    me = lax.axis_index("ty") * n_tx + lax.axis_index("tx")
    bits, summed = stages_of(n_ty, n_tx)
    half = keep + xor_permute(send, 1, total)
    done = [steps[0]()]
    half, done[0] = scatter_sum(half, me, bits, total, done[0])
    done.append(steps[1](*done))
    for pair in summed:
        half = direct_sum(half, pair, total)
    if steps[2:]:
        half, done[1] = lax.optimization_barrier((half, done[1]))
        done += [step(*done) for step in steps[2:]]
    half, done[-1] = gather(half, me, bits, total, done[-1])
    return half, xor_permute(half, 1, total), done


def per_device(n_ty, n_tx, table, object_field, probe, intensities, positions):
    win, modes = probe.shape[-1], probe.shape[1]
    margin, tile, scans = win // 2, object_field.shape[-1], positions.shape[2]
    spots = positions.reshape(scans, 2)
    measured = intensities.reshape(scans, win, win)
    match_y, match_x = pairings(n_ty), pairings(n_tx)
    n_y, n_x = len(match_y), len(match_x)
    odd_y = lax.axis_index("ty") % 2

    def swap(x, pairs_y, pairs_x):
        return lax.ppermute(x, AXES, flat_pairs(pairs_y, pairs_x, n_ty, n_tx))

    def rows_for(x, i, count, low, high):
        start = jnp.where(odd_y == i, high, low)
        return lax.dynamic_slice_in_dim(x, start, count, 1)

    tx_in = [swap(object_field, None, px) for px in match_x]
    rims = [rows_for(object_field, i, margin, 0, tile - margin) for i in range(n_y)]
    ty_in = [swap(rims[i], py, None) for i, py in enumerate(match_y)]
    corners = []
    for i, py in enumerate(match_y):
        corners += [swap(ty_in[i], None, px) for px in match_x[:1]]
        corners += [swap(rims[i], py, px) for px in match_x[1:]]

    shape_of = lambda x: jax.ShapeDtypeStruct(x.shape, x.dtype)
    ready = (probe, measured, jnp.asarray(table))
    ready = call(prepare_kernel, [shape_of(x) for x in ready], ready)
    (tx_in, ty_in, corners), (probe, root, table) = lax.optimization_barrier(
        ((tx_in, ty_in, corners), tuple(ready))
    )

    at_y, at_x = lax.axis_index("ty"), lax.axis_index("tx")
    half_shape = (modes, win + WEIGHT_ROWS, win)
    grid_shape = (2, 2 * tile + SUBLANES, 2 * tile)
    sent = [half_shape] * 2 + [object_field.shape] * 2 + [(2, 2, margin, tile)] * n_y
    scratch = [grid_shape, (2 * modes, win, win)]

    def exchanges(overlaps, rims):
        def folded(received):
            halves = [x.reshape(2, 2, margin, tile) for x in overlaps]
            place = lax.broadcasted_iota(jnp.int32, (1, 2, 1, 1), 1)
            for i, y in enumerate(received):
                here = place == jnp.where(odd_y == i, 1, 0)
                for k in (0, 1):
                    extra = if_paired(y[k][:, None], at_y, n_ty, i)
                    halves[k] = halves[k] + jnp.where(here, extra, 0.0)
            return [x.reshape(object_field.shape) for x in halves]

        def fold():
            return [swap(rim, py, None) for rim, py in zip(rims, match_y)]

        def across(received):
            mine = folded(received)
            return mine, [swap(x, None, px) for x, px in zip(mine, match_x)]

        def halo(received, columns):
            mine, theirs = columns
            total = list(mine)
            for i, x in enumerate(theirs):
                total[i] = total[i] + if_paired(x, at_x, n_tx, i)
            bands = [
                jnp.stack([rows_for(x, i, margin, 0, tile - margin) for x in total])
                for i in range(n_y)
            ]
            return [swap(band, py, None) for band, py in zip(bands, match_y)]

        return fold, across, halo

    ext, keep, send, first, second, *rims = call(
        functools.partial(first_kernel, n_ty, n_tx, n_y, n_x, margin),
        [grid_shape] + sent,
        [spots, object_field, probe, root, table, *ty_in, *tx_in, *corners],
        scratch,
    )
    steps = exchanges([first, second], rims)
    own, other, (_, (overlaps, tx_in), halo) = summed_halves(keep, send, n_ty, n_tx, steps)
    tile_mid, probe_mid, keep, send, first, second, *rims = call(
        functools.partial(second_kernel, n_ty, n_tx, n_y, n_x, margin),
        [object_field.shape, probe.shape] + sent,
        [spots, ext, *overlaps, probe, root, table, own, other, *tx_in, *halo],
        [grid_shape] + scratch,
    )
    steps = exchanges([first, second], rims)
    own, other, (_, (overlaps, tx_in)) = summed_halves(keep, send, n_ty, n_tx, steps[:2])
    return call(
        functools.partial(last_kernel, n_tx, n_x, margin),
        [object_field.shape, probe.shape],
        [tile_mid, *overlaps, probe_mid, own, other, *tx_in],
    )


def solution(mesh):
    n_ty, n_tx = mesh.shape["ty"], mesh.shape["tx"]
    placed = (P(None, "ty", "tx"), P(), P("ty", "tx", None, None, None), P("ty", "tx", None, None))

    def run(object_field, probe, intensities, positions):
        table = dft_table(probe.shape[-1])
        return jax.shard_map(
            functools.partial(per_device, n_ty, n_tx, table),
            mesh=mesh,
            in_specs=placed,
            out_specs=(P(None, "ty", "tx"), P()),
            check_vma=False,
        )(object_field, probe, intensities, positions)

    return run
```

```python
import functools

import jax
import jax.numpy as jnp
import numpy as np
from jax import lax
from jax.experimental import pallas as pl
from jax.experimental.pallas import tpu as pltpu
from jax.sharding import PartitionSpec as P

ROUNDS = 2
OBJECT_STEP = 0.1
PROBE_RELAX = 0.5
AXES = ("ty", "tx")
SUBLANES = 8
WEIGHT_ROWS = SUBLANES
F32 = jnp.float32
BF16 = jnp.bfloat16


def pairings(size):
    found = []
    for first in (0, 1):
        pairs = {}
        for low in range(first, size - 1, 2):
            pairs[low], pairs[low + 1] = low + 1, low
        if pairs:
            found.append(pairs)
    return found


def flat_pairs(pairs_y, pairs_x, n_ty, n_tx):
    out, alone = [], []
    for x in range(n_tx):
        for y in range(n_ty):
            to_y = y if pairs_y is None else pairs_y.get(y)
            to_x = x if pairs_x is None else pairs_x.get(x)
            if to_y is None or to_x is None:
                alone.append(y * n_tx + x)
            else:
                out.append((y * n_tx + x, to_y * n_tx + to_x))
    for a, b in zip(alone[::2], alone[1::2]):
        out += [(a, b), (b, a)]
    if len(alone) % 2:
        out.append((alone[-1], alone[-1]))
    return out


def if_paired(x, at, size, i):
    last = i + 2 * ((size - i) // 2)
    if i > 0:
        x = jnp.where(at >= i, x, 0.0)
    return jnp.where(at < last, x, 0.0) if last < size else x


def xor_permute(x, mask, total):
    return lax.ppermute(x, AXES, [(i, i ^ mask) for i in range(total)])


def split(x):
    high = x.astype(BF16)
    return high, (x - high.astype(F32)).astype(BF16)


def product(a, b):
    (a_high, a_low), (b_high, b_low) = a, b
    return jnp.dot(
        jnp.concatenate([a_high, a_low, a_high], axis=1),
        jnp.concatenate([b_high, b_high, b_low], axis=0),
        preferred_element_type=F32,
    )


def block(c, upper, lower):
    return jnp.concatenate(
        [jnp.concatenate([c, upper], axis=1), jnp.concatenate([lower, c], axis=1)], axis=0
    )


def lane_pick(width, margin, flag):
    lane = lax.broadcasted_iota(jnp.int32, (8, width), 1)
    below = jnp.where(lane < margin, 0, 1)
    return below == flag


def rowwise(mask, rows):
    return jnp.broadcast_to(mask[:1], (rows, mask.shape[1]))


def by_parity(odd, even_value, odd_value):
    return jnp.where(odd == 1, odd_value, even_value)


def compute(
    ext_ref, probe_ref, root_ref, pos_ref, table_ref, grid_ref, grad_ref, *, margin
):
    scans, win = root_ref.shape[0], root_ref.shape[1]
    modes = probe_ref.shape[1]
    width, tall = 2 * win, win + SUBLANES
    w_fwd = [block(table_ref[i], -table_ref[i + 1], table_ref[i + 1]) for i in (0, 2)]
    l_fwd = [block(table_ref[i], table_ref[i + 1], -table_ref[i + 1]) for i in (0, 2)]
    grid_ref[...] = jnp.zeros_like(grid_ref)
    windows, state, weights = {}, {}, []

    def corner(s):
        r, c = pos_ref[s, 0], pos_ref[s, 1]
        q = r % SUBLANES
        return pl.multiple_of(r - q, SUBLANES), q, c

    def enter(s):
        base, q, c = corner(s)
        turn = jnp.where(c <= margin, margin - c, margin + width - c)
        lift = jnp.where(q == 0, 0, tall - q)

        def window(part):
            band = pltpu.roll(ext_ref[part, pl.ds(base, tall), :], turn, 1)[:, :win]
            return pltpu.roll(band, lift, 0)[:win]

        o_re, o_im = windows[s] = window(0), window(1)
        power = o_re * o_re + o_im * o_im
        weights.append(jnp.sum(power.reshape(win // WEIGHT_ROWS, WEIGHT_ROWS, win), axis=0))
        rows = []
        for k in range(modes):
            p_re, p_im = probe_ref[0, k], probe_ref[1, k]
            rows.append(
                jnp.concatenate([p_re * o_re - p_im * o_im, p_re * o_im + p_im * o_re], axis=1)
            )
        state[s] = product(split(jnp.concatenate(rows, axis=0)), w_fwd)

    def forward(s):
        y = state[s]
        y = jnp.concatenate(
            [
                jnp.concatenate([y[k * win : (k + 1) * win, :win] for k in range(modes)], axis=1),
                jnp.concatenate([y[k * win : (k + 1) * win, win:] for k in range(modes)], axis=1),
            ],
            axis=0,
        )
        state[s] = product(l_fwd, split(y))

    def scale(s):
        far = state[s]
        square = far * far
        square = square[:win] + square[win:]
        total = square[:, :win]
        for k in range(1, modes):
            total = total + square[:, k * win : (k + 1) * win]
        ratio = root_ref[s] * lax.rsqrt(jnp.maximum(total, 1.0)) - 1.0
        ratio = jnp.concatenate([ratio] * modes, axis=1)
        far = far * jnp.concatenate([ratio, ratio], axis=0)
        state[s] = product(w_fwd, split(far))

    def backward(s):
        u = state[s]
        u = jnp.concatenate(
            [
                jnp.concatenate(
                    [u[:win, k * win : (k + 1) * win], u[win:, k * win : (k + 1) * win]], axis=1
                )
                for k in range(modes)
            ],
            axis=0,
        )
        state[s] = product(split(u), l_fwd)

    def leave(s):
        chi = state[s]
        o_re, o_im = windows[s]
        g_re = g_im = None
        for k in range(modes):
            p_re, p_im = probe_ref[0, k], probe_ref[1, k]
            c_re, c_im = chi[k * win : (k + 1) * win, :win], chi[k * win : (k + 1) * win, win:]
            a, b = p_re * c_re + p_im * c_im, p_re * c_im - p_im * c_re
            g_re, g_im = (a, b) if k == 0 else (g_re + a, g_im + b)
            a, b = o_re * c_re + o_im * c_im, o_re * c_im - o_im * c_re
            if s == 0:
                grad_ref[k], grad_ref[modes + k] = a, b
            else:
                grad_ref[k] += a
                grad_ref[modes + k] += b
        base, q, c = corner(s)
        back = jnp.where(c >= margin, c - margin, c + width - margin)
        for part, g in ((0, g_re), (1, g_im)):
            g = pltpu.roll(jnp.concatenate([g, jnp.zeros((SUBLANES, win), F32)], axis=0), q, 0)
            g = jnp.concatenate([g, jnp.zeros_like(g)], axis=1)
            grid_ref[part, pl.ds(base, tall), :] += pltpu.roll(g, back, 1)

    stages = (enter, forward, scale, backward, leave)
    for stage in stages:
        for s in range(scans):
            stage(s)
    return functools.reduce(jnp.add, weights)


def emit(grad_ref, weight, grid_ref, keep_ref, send_ref, first_ref, second_ref, rim_refs, margin):
    count, win = keep_ref.shape[0], grad_ref.shape[1]
    odd_y, odd_x = lax.axis_index("ty") % 2, lax.axis_index("tx") % 2
    for j in range(count):
        keep_ref[j, :win, :] = grad_ref[odd_x * count + j]
        send_ref[j, :win, :] = grad_ref[(1 - odd_x) * count + j]
        keep_ref[j, win:, :] = weight
        send_ref[j, win:, :] = weight
    tile = first_ref.shape[-1]
    mask = rowwise(lane_pick(tile, margin, odd_x), tile)
    for part in (0, 1):
        rows = grid_ref[part, margin : margin + tile, :]
        first_ref[part], second_ref[part] = chosen(mask, rows[:, tile:], rows[:, :tile])
        for i, ref in enumerate(rim_refs):
            start = pl.multiple_of(jnp.where(odd_y == i, 2 * tile - margin, 0), margin)
            rows = grid_ref[part, pl.ds(start, margin), :]
            ref[0, part], ref[1, part] = chosen(mask[:margin], rows[:, tile:], rows[:, :tile])


def chosen(mask, a, b):
    return jnp.where(mask, a, b), jnp.where(mask, b, a)


def prepare_kernel(probe_ref, meas_ref, probe_out, root_ref, table_ref):
    probe_out[...] = probe_ref[...]
    root_ref[...] = jnp.sqrt(meas_ref[...])
    win = probe_ref.shape[-1]
    line = lax.broadcasted_iota(jnp.int32, (win, win), 0)
    product_of = line * lax.broadcasted_iota(jnp.int32, (win, win), 1) % win
    angle = product_of.astype(F32) * (2.0 * np.pi / win)
    for i, values in enumerate((jnp.cos(angle), jnp.sin(angle))):
        table_ref[i], table_ref[i + 2] = split(values * win**-0.5)


def first_kernel(n_ty, n_tx, n_y, n_x, margin, pos_ref, obj_ref, probe_ref, root_ref, table_ref, *rest):
    take = iter(rest)
    ty_refs = [next(take) for _ in range(n_y)]
    tx_refs = [next(take) for _ in range(n_x)]
    corner_refs = [[next(take) for _ in range(n_x)] for _ in range(n_y)]
    ext_ref, keep_ref, send_ref, first_ref, second_ref, *rim_refs = take
    *rim_refs, grid_ref, grad_ref = rim_refs
    tile = obj_ref.shape[-1]
    at_y, at_x = lax.axis_index("ty"), lax.axis_index("tx")
    odd_y, odd_x = at_y % 2, at_x % 2
    pick = lane_pick(tile, margin, odd_x)

    def side(refs, part, rows):
        both = [if_paired(ref[part], at_x, n_tx, i) for i, ref in enumerate(refs)]
        both += [jnp.zeros((rows, tile), F32)] * (2 - n_x)
        return jnp.where(rowwise(pick, rows), both[0], both[1])

    for part in (0, 1):
        ext_ref[part, margin : margin + tile, :tile] = obj_ref[part]
        ext_ref[part, margin : margin + tile, tile:] = side(tx_refs, part, tile)
        bands = [
            if_paired(
                jnp.concatenate([ty_refs[i][part], side(corner_refs[i], part, margin)], axis=1),
                at_y, n_ty, i,
            )
            for i in range(n_y)
        ]
        bands += [jnp.zeros((margin, 2 * tile), F32)] * (2 - n_y)
        ext_ref[part, :margin, :] = by_parity(odd_y, bands[1], bands[0])
        ext_ref[part, margin + tile : 2 * tile, :] = by_parity(odd_y, bands[0], bands[1])
    weight = compute(
        ext_ref, probe_ref, root_ref, pos_ref, table_ref, grid_ref, grad_ref, margin=margin
    )
    emit(
        grad_ref, weight, grid_ref, keep_ref, send_ref, first_ref, second_ref, rim_refs, margin
    )


def combined_probe(probe_ref, own_ref, other_ref, new_ref, half):
    count, win, modes = own_ref.shape[0], probe_ref.shape[-1], probe_ref.shape[1]
    weight = jnp.sum(own_ref[0, win:, :])
    scale = PROBE_RELAX * win * win / jnp.full((8, win), weight, F32)
    scale = jnp.broadcast_to(scale[:1], (win, win))
    for j in range(count):
        for ref, index in ((own_ref, half * count + j), (other_ref, (1 - half) * count + j)):
            part, k = index // modes, index % modes
            new_ref[part, k] = probe_ref[part, k] + scale * ref[j, :win, :]


def second_kernel(
    n_ty, n_tx, n_y, n_x, margin, pos_ref, old_ref, first_ref, second_ref, probe_ref, root_ref,
    table_ref, own_ref, other_ref, *rest
):
    take = iter(rest)
    tx_refs = [next(take) for _ in range(n_x)]
    halo_refs = [next(take) for _ in range(n_y)]
    tile_ref, new_ref, keep_ref, send_ref, next_first_ref, next_second_ref, *rim_refs = take
    *rim_refs, ext_ref, grid_ref, grad_ref = rim_refs
    tile = probe_ref.shape[-1]
    at_y, at_x = lax.axis_index("ty"), lax.axis_index("tx")
    odd_y, odd_x = at_y % 2, at_x % 2
    combined_probe(probe_ref, own_ref, other_ref, new_ref, odd_x)
    row = lax.broadcasted_iota(jnp.int32, (2 * tile, 2 * tile), 0)
    lane = lax.broadcasted_iota(jnp.int32, (2 * tile, 2 * tile), 1)
    inside = (row >= jnp.where(at_y == 0, margin, 0)) & (
        row < jnp.where(at_y == n_ty - 1, margin + tile, 2 * tile)
    )
    inside &= (lane < jnp.where(at_x == n_tx - 1, tile, tile + margin)) | (
        lane >= jnp.where(at_x == 0, 2 * tile, tile + margin)
    )
    mask = rowwise(lane_pick(tile, margin, odd_x), tile)
    for i in range(2):
        start = pl.multiple_of(jnp.where(odd_y == i, margin + tile, 0), margin)
        for part in (0, 1):
            if i < n_y:
                ref = halo_refs[i]
                own, margins = chosen(mask[:margin], ref[1, part], ref[0, part])
                rows = jnp.concatenate([own, margins], axis=1)
            else:
                rows = jnp.zeros((margin, 2 * tile), F32)
            ext_ref[part, pl.ds(start, margin), :] = rows
    for part in (0, 1):
        both = [first_ref[part], second_ref[part]]
        for i, ref in enumerate(tx_refs):
            both[i] = both[i] + if_paired(ref[part], at_x, n_tx, i)
        own, margins = chosen(mask, both[1], both[0])
        ext_ref[part, margin : margin + tile, :] = jnp.concatenate([own, margins], axis=1)
        step = jnp.where(inside, OBJECT_STEP * ext_ref[part, : 2 * tile, :], 0.0)
        ext_ref[part, : 2 * tile, :] = old_ref[part, : 2 * tile, :] + step
        tile_ref[part] = ext_ref[part, margin : margin + tile, :tile]
    weight = compute(
        ext_ref, new_ref, root_ref, pos_ref, table_ref, grid_ref, grad_ref, margin=margin
    )
    emit(
        grad_ref, weight, grid_ref, keep_ref, send_ref, next_first_ref, next_second_ref, rim_refs,
        margin,
    )


def last_kernel(
    n_tx, n_x, margin, tile_ref, first_ref, second_ref, probe_ref, own_ref, other_ref, *rest
):
    *tx_refs, obj_ref, new_ref = rest
    tile = tile_ref.shape[-1]
    at_x = lax.axis_index("tx")
    combined_probe(probe_ref, own_ref, other_ref, new_ref, at_x % 2)
    mask = rowwise(lane_pick(tile, margin, at_x % 2), tile)
    for part in (0, 1):
        both = [first_ref[part], second_ref[part]]
        for i, ref in enumerate(tx_refs):
            both[i] = both[i] + if_paired(ref[part], at_x, n_tx, i)
        obj_ref[part] = tile_ref[part] + OBJECT_STEP * chosen(mask, both[1], both[0])[0]


def call(kernel, outs, ins, scratch=()):
    smem = pl.BlockSpec(memory_space=pltpu.SMEM)
    vmem = pl.BlockSpec(memory_space=pltpu.VMEM)
    shapes = [s if hasattr(s, "dtype") else jax.ShapeDtypeStruct(s, F32) for s in outs]
    return pl.pallas_call(
        kernel,
        out_shape=shapes,
        in_specs=[smem if x.dtype == jnp.int32 else vmem for x in ins],
        out_specs=[vmem] * len(outs),
        scratch_shapes=[pltpu.VMEM(s, F32) for s in scratch],
        compiler_params=pltpu.CompilerParams(vmem_limit_bytes=16 * 1024 * 1024),
    )(*ins)


def bit_of(me, bit):
    return (me >> bit) & 1


def mask_of(bits, m):
    return sum(((m >> i) & 1) << b for i, b in enumerate(bits))


def swap_over(x, bits, m, total):
    masks = [mask_of(b, m) for b in bits]
    return lax.ppermute(x, AXES, [(i, i ^ masks[i & 1]) for i in range(total)])


def local_index(me, bits):
    even, odd = (sum(bit_of(me, b) << i for i, b in enumerate(side)) for side in bits)
    return even if bits[0] == bits[1] else jnp.where(me & 1 == 0, even, odd)


def tree(values):
    while len(values) > 1:
        values = [a + b for a, b in zip(values[::2], values[1::2])] + values[len(values) & ~1 :]
    return values[0]


def scatter_sum(x, me, bits, total, beside):
    here = local_index(me, bits)
    n = 1 << len(bits[0])
    x = x.reshape((n, x.shape[0] // n) + x.shape[1:])
    parts = [lax.dynamic_index_in_dim(x, here, 0, False)]
    for m in range(1, n):
        part = lax.dynamic_index_in_dim(x, here ^ m, 0, False)
        parts.append(swap_over(part, bits, m, total))
    parts[0], beside = lax.optimization_barrier((parts[0], beside))
    return tree(parts), beside


def direct_sum(x, bits, total):
    return tree([x] + [swap_over(x, bits, m, total) for m in range(1, 1 << len(bits[0]))])


def gather(x, me, bits, total, beside):
    here = local_index(me, bits)
    n = 1 << len(bits[0])
    parts = [swap_over(x, bits, m, total) for m in range(1, n)]
    x, beside = lax.optimization_barrier((x, beside))
    parts = jnp.stack([x] + parts)
    whole = [lax.dynamic_index_in_dim(parts, here ^ j, 0, False) for j in range(n)]
    return jnp.concatenate(whole), beside


def stages_of(n_ty, n_tx):
    levels, tx_bits = (n_ty * n_tx).bit_length() - 1, n_tx.bit_length() - 1
    near = tuple(b for b in dict.fromkeys((tx_bits, 1)) if b < levels)
    rest = [b for b in range(1, levels) if b not in near]
    far = tuple(rest[:2])
    if len(near) == len(far):
        return (near, far), [(far, near)] + [((b,), (b,)) for b in rest[2:]]
    return (near, near), [((b,), (b,)) for b in rest]


def summed_halves(keep, send, n_ty, n_tx, steps):
    total = n_ty * n_tx
    me = lax.axis_index("ty") * n_tx + lax.axis_index("tx")
    bits, summed = stages_of(n_ty, n_tx)
    half = keep + xor_permute(send, 1, total)
    done = [steps[0]()]
    half, done[0] = scatter_sum(half, me, bits, total, done[0])
    done.append(steps[1](*done))
    for pair in summed:
        half = direct_sum(half, pair, total)
    if steps[2:]:
        half, done[1] = lax.optimization_barrier((half, done[1]))
        done += [step(*done) for step in steps[2:]]
    half, done[-1] = gather(half, me, bits, total, done[-1])
    return half, xor_permute(half, 1, total), done


def per_device(n_ty, n_tx, object_field, probe, intensities, positions):
    win, modes = probe.shape[-1], probe.shape[1]
    margin, tile, scans = win // 2, object_field.shape[-1], positions.shape[2]
    spots = positions.reshape(scans, 2)
    measured = intensities.reshape(scans, win, win)
    match_y, match_x = pairings(n_ty), pairings(n_tx)
    n_y, n_x = len(match_y), len(match_x)
    odd_y = lax.axis_index("ty") % 2

    def swap(x, pairs_y, pairs_x):
        return lax.ppermute(x, AXES, flat_pairs(pairs_y, pairs_x, n_ty, n_tx))

    def rows_for(x, i, count, low, high):
        start = jnp.where(odd_y == i, high, low)
        return lax.dynamic_slice_in_dim(x, start, count, 1)

    tx_in = [swap(object_field, None, px) for px in match_x]
    rims = [rows_for(object_field, i, margin, 0, tile - margin) for i in range(n_y)]
    ty_in = [swap(rims[i], py, None) for i, py in enumerate(match_y)]
    corners = []
    for i, py in enumerate(match_y):
        corners += [swap(ty_in[i], None, px) for px in match_x[:1]]
        corners += [swap(rims[i], py, px) for px in match_x[1:]]

    shape_of = lambda x: jax.ShapeDtypeStruct(x.shape, x.dtype)
    outs = [shape_of(probe), shape_of(measured), jax.ShapeDtypeStruct((4, win, win), BF16)]
    ready = call(prepare_kernel, outs, (probe, measured))
    ty_in, ready = lax.optimization_barrier((ty_in, ready))
    for i, rim in enumerate(ty_in[: len(match_y) if match_x else 0]):
        corners[i * n_x] = swap(rim, None, match_x[0])
    (tx_in, ty_in, corners), (probe, root, table) = lax.optimization_barrier(
        ((tx_in, ty_in, corners), tuple(ready))
    )

    at_y, at_x = lax.axis_index("ty"), lax.axis_index("tx")
    half_shape = (modes, win + WEIGHT_ROWS, win)
    grid_shape = (2, 2 * tile + SUBLANES, 2 * tile)
    sent = [half_shape] * 2 + [object_field.shape] * 2 + [(2, 2, margin, tile)] * n_y
    scratch = [grid_shape, (2 * modes, win, win)]

    def exchanges(overlaps, rims):
        def folded(received):
            halves = [x.reshape(2, 2, margin, tile) for x in overlaps]
            place = lax.broadcasted_iota(jnp.int32, (1, 2, 1, 1), 1)
            for i, y in enumerate(received):
                here = place == jnp.where(odd_y == i, 1, 0)
                for k in (0, 1):
                    extra = if_paired(y[k][:, None], at_y, n_ty, i)
                    halves[k] = halves[k] + jnp.where(here, extra, 0.0)
            return [x.reshape(object_field.shape) for x in halves]

        def fold():
            return [swap(rim, py, None) for rim, py in zip(rims, match_y)]

        def across(received):
            mine = folded(received)
            return mine, [swap(x, None, px) for x, px in zip(mine, match_x)]

        def halo(received, columns):
            mine, theirs = columns
            total = list(mine)
            for i, x in enumerate(theirs):
                total[i] = total[i] + if_paired(x, at_x, n_tx, i)
            bands = [
                jnp.stack([rows_for(x, i, margin, 0, tile - margin) for x in total])
                for i in range(n_y)
            ]
            return [swap(band, py, None) for band, py in zip(bands, match_y)]

        return fold, across, halo

    ext, keep, send, first, second, *rims = call(
        functools.partial(first_kernel, n_ty, n_tx, n_y, n_x, margin),
        [grid_shape] + sent,
        [spots, object_field, probe, root, table, *ty_in, *tx_in, *corners],
        scratch,
    )
    steps = exchanges([first, second], rims)
    own, other, (_, (overlaps, tx_in), halo) = summed_halves(keep, send, n_ty, n_tx, steps)
    tile_mid, probe_mid, keep, send, first, second, *rims = call(
        functools.partial(second_kernel, n_ty, n_tx, n_y, n_x, margin),
        [object_field.shape, probe.shape] + sent,
        [spots, ext, *overlaps, probe, root, table, own, other, *tx_in, *halo],
        [grid_shape] + scratch,
    )
    steps = exchanges([first, second], rims)
    own, other, (_, (overlaps, tx_in)) = summed_halves(keep, send, n_ty, n_tx, steps[:2])
    return call(
        functools.partial(last_kernel, n_tx, n_x, margin),
        [object_field.shape, probe.shape],
        [tile_mid, *overlaps, probe_mid, own, other, *tx_in],
    )


def solution(mesh):
    n_ty, n_tx = mesh.shape["ty"], mesh.shape["tx"]
    placed = (P(None, "ty", "tx"), P(), P("ty", "tx", None, None, None), P("ty", "tx", None, None))

    def run(object_field, probe, intensities, positions):
        return jax.shard_map(
            functools.partial(per_device, n_ty, n_tx),
            mesh=mesh,
            in_specs=placed,
            out_specs=(P(None, "ty", "tx"), P()),
            check_vma=False,
        )(object_field, probe, intensities, positions)

    return run
```

```python
import functools

import jax
import jax.numpy as jnp
import numpy as np
from jax import lax
from jax.experimental import pallas as pl
from jax.experimental.pallas import tpu as pltpu
from jax.sharding import PartitionSpec as P

ROUNDS = 2
OBJECT_STEP = 0.1
PROBE_RELAX = 0.5
AXES = ("ty", "tx")
SUBLANES = 8
WEIGHT_ROWS = SUBLANES
F32 = jnp.float32
BF16 = jnp.bfloat16


def pairings(size):
    found = []
    for first in (0, 1):
        pairs = {}
        for low in range(first, size - 1, 2):
            pairs[low], pairs[low + 1] = low + 1, low
        if pairs:
            found.append(pairs)
    return found


def flat_pairs(pairs_y, pairs_x, n_ty, n_tx):
    out, alone = [], []
    for x in range(n_tx):
        for y in range(n_ty):
            to_y = y if pairs_y is None else pairs_y.get(y)
            to_x = x if pairs_x is None else pairs_x.get(x)
            if to_y is None or to_x is None:
                alone.append(y * n_tx + x)
            else:
                out.append((y * n_tx + x, to_y * n_tx + to_x))
    for a, b in zip(alone[::2], alone[1::2]):
        out += [(a, b), (b, a)]
    if len(alone) % 2:
        out.append((alone[-1], alone[-1]))
    return out


def if_paired(x, at, size, i):
    last = i + 2 * ((size - i) // 2)
    if i > 0:
        x = jnp.where(at >= i, x, 0.0)
    return jnp.where(at < last, x, 0.0) if last < size else x


def xor_permute(x, mask, total):
    return lax.ppermute(x, AXES, [(i, i ^ mask) for i in range(total)])


def split(x):
    high = x.astype(BF16)
    return high, (x - high.astype(F32)).astype(BF16)


def product(a, b):
    (a_high, a_low), (b_high, b_low) = a, b
    return jnp.dot(
        jnp.concatenate([a_high, a_low, a_high], axis=1),
        jnp.concatenate([b_high, b_high, b_low], axis=0),
        preferred_element_type=F32,
    )


def block(c, upper, lower):
    return jnp.concatenate(
        [jnp.concatenate([c, upper], axis=1), jnp.concatenate([lower, c], axis=1)], axis=0
    )


def lane_pick(width, margin, flag):
    lane = lax.broadcasted_iota(jnp.int32, (8, width), 1)
    below = jnp.where(lane < margin, 0, 1)
    return below == flag


def rowwise(mask, rows):
    return jnp.broadcast_to(mask[:1], (rows, mask.shape[1]))


def by_parity(odd, even_value, odd_value):
    return jnp.where(odd == 1, odd_value, even_value)


def compute(
    ext_ref, probe_ref, root_ref, pos_ref, table_ref, grid_ref, grad_ref, *, margin
):
    scans, win = root_ref.shape[0], root_ref.shape[1]
    modes = probe_ref.shape[1]
    width, tall = 2 * win, win + SUBLANES
    w_fwd = [block(table_ref[i], -table_ref[i + 1], table_ref[i + 1]) for i in (0, 2)]
    l_fwd = [block(table_ref[i], table_ref[i + 1], -table_ref[i + 1]) for i in (0, 2)]
    grid_ref[...] = jnp.zeros_like(grid_ref)
    windows, state, weights = {}, {}, []

    def corner(s):
        r, c = pos_ref[s, 0], pos_ref[s, 1]
        q = r % SUBLANES
        return pl.multiple_of(r - q, SUBLANES), q, c

    def enter(s):
        base, q, c = corner(s)
        turn = jnp.where(c <= margin, margin - c, margin + width - c)
        lift = jnp.where(q == 0, 0, tall - q)

        def window(part):
            band = pltpu.roll(ext_ref[part, pl.ds(base, tall), :], turn, 1)[:, :win]
            return pltpu.roll(band, lift, 0)[:win]

        o_re, o_im = windows[s] = window(0), window(1)
        power = o_re * o_re + o_im * o_im
        weights.append(jnp.sum(power.reshape(win // WEIGHT_ROWS, WEIGHT_ROWS, win), axis=0))
        rows = []
        for k in range(modes):
            p_re, p_im = probe_ref[0, k], probe_ref[1, k]
            rows.append(
                jnp.concatenate([p_re * o_re - p_im * o_im, p_re * o_im + p_im * o_re], axis=1)
            )
        state[s] = product(split(jnp.concatenate(rows, axis=0)), w_fwd)

    def forward(s):
        y = state[s]
        y = jnp.concatenate(
            [
                jnp.concatenate([y[k * win : (k + 1) * win, :win] for k in range(modes)], axis=1),
                jnp.concatenate([y[k * win : (k + 1) * win, win:] for k in range(modes)], axis=1),
            ],
            axis=0,
        )
        state[s] = product(l_fwd, split(y))

    def scale(s):
        far = state[s]
        square = far * far
        square = square[:win] + square[win:]
        total = square[:, :win]
        for k in range(1, modes):
            total = total + square[:, k * win : (k + 1) * win]
        ratio = root_ref[s] * lax.rsqrt(jnp.maximum(total, 1.0)) - 1.0
        ratio = jnp.concatenate([ratio] * modes, axis=1)
        far = far * jnp.concatenate([ratio, ratio], axis=0)
        state[s] = product(w_fwd, split(far))

    def backward(s):
        u = state[s]
        u = jnp.concatenate(
            [
                jnp.concatenate(
                    [u[:win, k * win : (k + 1) * win], u[win:, k * win : (k + 1) * win]], axis=1
                )
                for k in range(modes)
            ],
            axis=0,
        )
        state[s] = product(split(u), l_fwd)

    def leave(s):
        chi = state[s]
        o_re, o_im = windows[s]
        g_re = g_im = None
        for k in range(modes):
            p_re, p_im = probe_ref[0, k], probe_ref[1, k]
            c_re, c_im = chi[k * win : (k + 1) * win, :win], chi[k * win : (k + 1) * win, win:]
            a, b = p_re * c_re + p_im * c_im, p_re * c_im - p_im * c_re
            g_re, g_im = (a, b) if k == 0 else (g_re + a, g_im + b)
            a, b = o_re * c_re + o_im * c_im, o_re * c_im - o_im * c_re
            if s == 0:
                grad_ref[k], grad_ref[modes + k] = a, b
            else:
                grad_ref[k] += a
                grad_ref[modes + k] += b
        base, q, c = corner(s)
        back = jnp.where(c >= margin, c - margin, c + width - margin)
        for part, g in ((0, g_re), (1, g_im)):
            g = pltpu.roll(jnp.concatenate([g, jnp.zeros((SUBLANES, win), F32)], axis=0), q, 0)
            g = jnp.concatenate([g, jnp.zeros_like(g)], axis=1)
            grid_ref[part, pl.ds(base, tall), :] += pltpu.roll(g, back, 1)

    stages = (enter, forward, scale, backward, leave)
    for stage in stages:
        for s in range(scans):
            stage(s)
    return functools.reduce(jnp.add, weights)


def emit(grad_ref, weight, grid_ref, keep_ref, send_ref, first_ref, second_ref, rim_refs, margin):
    count, win = keep_ref.shape[0], grad_ref.shape[1]
    odd_y, odd_x = lax.axis_index("ty") % 2, lax.axis_index("tx") % 2
    for j in range(count):
        keep_ref[j, :win, :] = grad_ref[odd_x * count + j]
        send_ref[j, :win, :] = grad_ref[(1 - odd_x) * count + j]
        keep_ref[j, win:, :] = weight
        send_ref[j, win:, :] = weight
    tile = first_ref.shape[-1]
    mask = rowwise(lane_pick(tile, margin, odd_x), tile)
    for part in (0, 1):
        rows = grid_ref[part, margin : margin + tile, :]
        first_ref[part], second_ref[part] = chosen(mask, rows[:, tile:], rows[:, :tile])
        for i, ref in enumerate(rim_refs):
            start = pl.multiple_of(jnp.where(odd_y == i, 2 * tile - margin, 0), margin)
            rows = grid_ref[part, pl.ds(start, margin), :]
            ref[0, part], ref[1, part] = chosen(mask[:margin], rows[:, tile:], rows[:, :tile])


def chosen(mask, a, b):
    return jnp.where(mask, a, b), jnp.where(mask, b, a)


def prepare_kernel(probe_ref, meas_ref, probe_out, root_ref, table_ref):
    probe_out[...] = probe_ref[...]
    root_ref[...] = jnp.sqrt(meas_ref[...])
    win = probe_ref.shape[-1]
    line = lax.broadcasted_iota(jnp.int32, (win, win), 0)
    product_of = line * lax.broadcasted_iota(jnp.int32, (win, win), 1) % win
    angle = product_of.astype(F32) * (2.0 * np.pi / win)
    for i, values in enumerate((jnp.cos(angle), jnp.sin(angle))):
        table_ref[i], table_ref[i + 2] = split(values * win**-0.5)


def first_kernel(n_ty, n_tx, n_y, n_x, margin, pos_ref, obj_ref, probe_ref, root_ref, table_ref, *rest):
    take = iter(rest)
    ty_refs = [next(take) for _ in range(n_y)]
    tx_refs = [next(take) for _ in range(n_x)]
    corner_refs = [[next(take) for _ in range(n_x)] for _ in range(n_y)]
    ext_ref, keep_ref, send_ref, first_ref, second_ref, *rim_refs = take
    *rim_refs, grid_ref, grad_ref = rim_refs
    tile = obj_ref.shape[-1]
    at_y, at_x = lax.axis_index("ty"), lax.axis_index("tx")
    odd_y, odd_x = at_y % 2, at_x % 2
    pick = lane_pick(tile, margin, odd_x)

    def side(refs, part, rows):
        both = [if_paired(ref[part], at_x, n_tx, i) for i, ref in enumerate(refs)]
        both += [jnp.zeros((rows, tile), F32)] * (2 - n_x)
        return jnp.where(rowwise(pick, rows), both[0], both[1])

    for part in (0, 1):
        ext_ref[part, margin : margin + tile, :tile] = obj_ref[part]
        ext_ref[part, margin : margin + tile, tile:] = side(tx_refs, part, tile)
        bands = [
            if_paired(
                jnp.concatenate([ty_refs[i][part], side(corner_refs[i], part, margin)], axis=1),
                at_y, n_ty, i,
            )
            for i in range(n_y)
        ]
        bands += [jnp.zeros((margin, 2 * tile), F32)] * (2 - n_y)
        ext_ref[part, :margin, :] = by_parity(odd_y, bands[1], bands[0])
        ext_ref[part, margin + tile : 2 * tile, :] = by_parity(odd_y, bands[0], bands[1])
    weight = compute(
        ext_ref, probe_ref, root_ref, pos_ref, table_ref, grid_ref, grad_ref, margin=margin
    )
    emit(
        grad_ref, weight, grid_ref, keep_ref, send_ref, first_ref, second_ref, rim_refs, margin
    )


def combined_probe(probe_ref, own_ref, other_ref, new_ref, half):
    count, win, modes = own_ref.shape[0], probe_ref.shape[-1], probe_ref.shape[1]
    weight = jnp.sum(own_ref[0, win:, :])
    scale = PROBE_RELAX * win * win / jnp.full((8, win), weight, F32)
    scale = jnp.broadcast_to(scale[:1], (win, win))
    for j in range(count):
        for ref, index in ((own_ref, half * count + j), (other_ref, (1 - half) * count + j)):
            part, k = index // modes, index % modes
            new_ref[part, k] = probe_ref[part, k] + scale * ref[j, :win, :]


def second_kernel(
    n_ty, n_tx, n_y, n_x, margin, pos_ref, old_ref, first_ref, second_ref, probe_ref, root_ref,
    table_ref, own_ref, other_ref, *rest
):
    take = iter(rest)
    tx_refs = [next(take) for _ in range(n_x)]
    halo_refs = [next(take) for _ in range(n_y)]
    tile_ref, new_ref, keep_ref, send_ref, next_first_ref, next_second_ref, *rim_refs = take
    *rim_refs, ext_ref, grid_ref, grad_ref = rim_refs
    tile = probe_ref.shape[-1]
    at_y, at_x = lax.axis_index("ty"), lax.axis_index("tx")
    odd_y, odd_x = at_y % 2, at_x % 2
    combined_probe(probe_ref, own_ref, other_ref, new_ref, odd_x)
    row = lax.broadcasted_iota(jnp.int32, (2 * tile, 2 * tile), 0)
    lane = lax.broadcasted_iota(jnp.int32, (2 * tile, 2 * tile), 1)
    inside = (row >= jnp.where(at_y == 0, margin, 0)) & (
        row < jnp.where(at_y == n_ty - 1, margin + tile, 2 * tile)
    )
    inside &= (lane < jnp.where(at_x == n_tx - 1, tile, tile + margin)) | (
        lane >= jnp.where(at_x == 0, 2 * tile, tile + margin)
    )
    mask = rowwise(lane_pick(tile, margin, odd_x), tile)
    for i in range(2):
        start = pl.multiple_of(jnp.where(odd_y == i, margin + tile, 0), margin)
        for part in (0, 1):
            if i < n_y:
                ref = halo_refs[i]
                own, margins = chosen(mask[:margin], ref[1, part], ref[0, part])
                rows = jnp.concatenate([own, margins], axis=1)
            else:
                rows = jnp.zeros((margin, 2 * tile), F32)
            ext_ref[part, pl.ds(start, margin), :] = rows
    for part in (0, 1):
        both = [first_ref[part], second_ref[part]]
        for i, ref in enumerate(tx_refs):
            both[i] = both[i] + if_paired(ref[part], at_x, n_tx, i)
        own, margins = chosen(mask, both[1], both[0])
        ext_ref[part, margin : margin + tile, :] = jnp.concatenate([own, margins], axis=1)
        step = jnp.where(inside, OBJECT_STEP * ext_ref[part, : 2 * tile, :], 0.0)
        ext_ref[part, : 2 * tile, :] = old_ref[part, : 2 * tile, :] + step
        tile_ref[part] = ext_ref[part, margin : margin + tile, :tile]
    weight = compute(
        ext_ref, new_ref, root_ref, pos_ref, table_ref, grid_ref, grad_ref, margin=margin
    )
    emit(
        grad_ref, weight, grid_ref, keep_ref, send_ref, next_first_ref, next_second_ref, rim_refs,
        margin,
    )


def last_kernel(
    n_tx, n_x, margin, tile_ref, first_ref, second_ref, probe_ref, own_ref, other_ref, *rest
):
    *tx_refs, obj_ref, new_ref = rest
    tile = tile_ref.shape[-1]
    at_x = lax.axis_index("tx")
    combined_probe(probe_ref, own_ref, other_ref, new_ref, at_x % 2)
    mask = rowwise(lane_pick(tile, margin, at_x % 2), tile)
    for part in (0, 1):
        both = [first_ref[part], second_ref[part]]
        for i, ref in enumerate(tx_refs):
            both[i] = both[i] + if_paired(ref[part], at_x, n_tx, i)
        obj_ref[part] = tile_ref[part] + OBJECT_STEP * chosen(mask, both[1], both[0])[0]


def call(kernel, outs, ins, scratch=()):
    smem = pl.BlockSpec(memory_space=pltpu.SMEM)
    vmem = pl.BlockSpec(memory_space=pltpu.VMEM)
    shapes = [s if hasattr(s, "dtype") else jax.ShapeDtypeStruct(s, F32) for s in outs]
    return pl.pallas_call(
        kernel,
        out_shape=shapes,
        in_specs=[smem if x.dtype == jnp.int32 else vmem for x in ins],
        out_specs=[vmem] * len(outs),
        scratch_shapes=[pltpu.VMEM(s, F32) for s in scratch],
        compiler_params=pltpu.CompilerParams(vmem_limit_bytes=16 * 1024 * 1024),
    )(*ins)


def bit_of(me, bit):
    return (me >> bit) & 1


def mask_of(bits, m):
    return sum(((m >> i) & 1) << b for i, b in enumerate(bits))


def swap_over(x, bits, m, total):
    masks = [mask_of(b, m) for b in bits]
    return lax.ppermute(x, AXES, [(i, i ^ masks[i & 1]) for i in range(total)])


def local_index(me, bits):
    even, odd = (sum(bit_of(me, b) << i for i, b in enumerate(side)) for side in bits)
    return even if bits[0] == bits[1] else jnp.where(me & 1 == 0, even, odd)


def tree(values):
    while len(values) > 1:
        values = [a + b for a, b in zip(values[::2], values[1::2])] + values[len(values) & ~1 :]
    return values[0]


def scatter_sum(x, me, bits, total, beside):
    here = local_index(me, bits)
    n = 1 << len(bits[0])
    x = x.reshape((n, x.shape[0] // n) + x.shape[1:])
    parts = [lax.dynamic_index_in_dim(x, here, 0, False)]
    for m in range(1, n):
        part = lax.dynamic_index_in_dim(x, here ^ m, 0, False)
        parts.append(swap_over(part, bits, m, total))
    parts[0], beside = lax.optimization_barrier((parts[0], beside))
    return tree(parts), beside


def direct_sum(x, bits, total):
    return tree([x] + [swap_over(x, bits, m, total) for m in range(1, 1 << len(bits[0]))])


def gather(x, me, bits, total, beside):
    here = local_index(me, bits)
    n = 1 << len(bits[0])
    parts = [swap_over(x, bits, m, total) for m in range(1, n)]
    x, beside = lax.optimization_barrier((x, beside))
    parts = jnp.stack([x] + parts)
    whole = [lax.dynamic_index_in_dim(parts, here ^ j, 0, False) for j in range(n)]
    return jnp.concatenate(whole), beside


def stages_of(n_ty, n_tx):
    levels, tx_bits = (n_ty * n_tx).bit_length() - 1, n_tx.bit_length() - 1
    near = tuple(b for b in dict.fromkeys((tx_bits, 1)) if b < levels)
    rest = [b for b in range(1, levels) if b not in near]
    far = tuple(rest[:2])
    if len(near) == len(far):
        return (near, far[::-1]), [(far[::-1], near)] + [((b,), (b,)) for b in rest[2:]]
    return (near, near), [((b,), (b,)) for b in rest]


def summed_halves(keep, send, n_ty, n_tx, steps):
    total = n_ty * n_tx
    me = lax.axis_index("ty") * n_tx + lax.axis_index("tx")
    bits, summed = stages_of(n_ty, n_tx)
    half = keep + xor_permute(send, 1, total)
    done = [steps[0]()]
    half, done[0] = scatter_sum(half, me, bits, total, done[0])
    done.append(steps[1](*done))
    for pair in summed:
        half = direct_sum(half, pair, total)
    if steps[2:]:
        half, done[1] = lax.optimization_barrier((half, done[1]))
        done += [step(*done) for step in steps[2:]]
    half, done[-1] = gather(half, me, bits, total, done[-1])
    return half, xor_permute(half, 1, total), done


def per_device(n_ty, n_tx, object_field, probe, intensities, positions):
    win, modes = probe.shape[-1], probe.shape[1]
    margin, tile, scans = win // 2, object_field.shape[-1], positions.shape[2]
    spots = positions.reshape(scans, 2)
    measured = intensities.reshape(scans, win, win)
    match_y, match_x = pairings(n_ty), pairings(n_tx)
    n_y, n_x = len(match_y), len(match_x)
    odd_y = lax.axis_index("ty") % 2

    def swap(x, pairs_y, pairs_x):
        return lax.ppermute(x, AXES, flat_pairs(pairs_y, pairs_x, n_ty, n_tx))

    def rows_for(x, i, count, low, high):
        start = jnp.where(odd_y == i, high, low)
        return lax.dynamic_slice_in_dim(x, start, count, 1)

    tx_in = [swap(object_field, None, px) for px in match_x]
    rims = [rows_for(object_field, i, margin, 0, tile - margin) for i in range(n_y)]
    ty_in = [swap(rims[i], py, None) for i, py in enumerate(match_y)]
    corners = []
    for i, py in enumerate(match_y):
        corners += [swap(ty_in[i], None, px) for px in match_x[:1]]
        corners += [swap(rims[i], py, px) for px in match_x[1:]]

    shape_of = lambda x: jax.ShapeDtypeStruct(x.shape, x.dtype)
    outs = [shape_of(probe), shape_of(measured), jax.ShapeDtypeStruct((4, win, win), BF16)]
    ready = call(prepare_kernel, outs, (probe, measured))
    ty_in, ready = lax.optimization_barrier((ty_in, ready))
    for i, rim in enumerate(ty_in[: len(match_y) if match_x else 0]):
        corners[i * n_x] = swap(rim, None, match_x[0])
    (tx_in, ty_in, corners), (probe, root, table) = lax.optimization_barrier(
        ((tx_in, ty_in, corners), tuple(ready))
    )

    at_y, at_x = lax.axis_index("ty"), lax.axis_index("tx")
    half_shape = (modes, win + WEIGHT_ROWS, win)
    grid_shape = (2, 2 * tile + SUBLANES, 2 * tile)
    sent = [half_shape] * 2 + [object_field.shape] * 2 + [(2, 2, margin, tile)] * n_y
    scratch = [grid_shape, (2 * modes, win, win)]

    def exchanges(overlaps, rims):
        def folded(received):
            halves = [x.reshape(2, 2, margin, tile) for x in overlaps]
            place = lax.broadcasted_iota(jnp.int32, (1, 2, 1, 1), 1)
            for i, y in enumerate(received):
                here = place == jnp.where(odd_y == i, 1, 0)
                for k in (0, 1):
                    extra = if_paired(y[k][:, None], at_y, n_ty, i)
                    halves[k] = halves[k] + jnp.where(here, extra, 0.0)
            return [x.reshape(object_field.shape) for x in halves]

        def fold():
            return [swap(rim, py, None) for rim, py in zip(rims, match_y)]

        def across(received):
            mine = folded(received)
            return mine, [swap(x, None, px) for x, px in zip(mine, match_x)]

        def halo(received, columns):
            mine, theirs = columns
            total = list(mine)
            for i, x in enumerate(theirs):
                total[i] = total[i] + if_paired(x, at_x, n_tx, i)
            bands = [
                jnp.stack([rows_for(x, i, margin, 0, tile - margin) for x in total])
                for i in range(n_y)
            ]
            return [swap(band, py, None) for band, py in zip(bands, match_y)]

        return fold, across, halo

    ext, keep, send, first, second, *rims = call(
        functools.partial(first_kernel, n_ty, n_tx, n_y, n_x, margin),
        [grid_shape] + sent,
        [spots, object_field, probe, root, table, *ty_in, *tx_in, *corners],
        scratch,
    )
    steps = exchanges([first, second], rims)
    own, other, (_, (overlaps, tx_in), halo) = summed_halves(keep, send, n_ty, n_tx, steps)
    tile_mid, probe_mid, keep, send, first, second, *rims = call(
        functools.partial(second_kernel, n_ty, n_tx, n_y, n_x, margin),
        [object_field.shape, probe.shape] + sent,
        [spots, ext, *overlaps, probe, root, table, own, other, *tx_in, *halo],
        [grid_shape] + scratch,
    )
    steps = exchanges([first, second], rims)
    own, other, (_, (overlaps, tx_in)) = summed_halves(keep, send, n_ty, n_tx, steps[:2])
    return call(
        functools.partial(last_kernel, n_tx, n_x, margin),
        [object_field.shape, probe.shape],
        [tile_mid, *overlaps, probe_mid, own, other, *tx_in],
    )


def solution(mesh):
    n_ty, n_tx = mesh.shape["ty"], mesh.shape["tx"]
    placed = (P(None, "ty", "tx"), P(), P("ty", "tx", None, None, None), P("ty", "tx", None, None))

    def run(object_field, probe, intensities, positions):
        return jax.shard_map(
            functools.partial(per_device, n_ty, n_tx),
            mesh=mesh,
            in_specs=placed,
            out_specs=(P(None, "ty", "tx"), P()),
            check_vma=False,
        )(object_field, probe, intensities, positions)

    return run
```
